128 devices in a mesh: pipe: 4 (over y), dp: 32 (over x, z, core).
Axes of the slice: x: 4, y: 4, z: 4, core: 2. Of those that a mesh axis runs over, the one named last changes fastest.
Arguments:
- acts: bfloat16 [4, 16384, 8192], P('pipe', 'dp'), may hold values from -6 to 6
- output_gradient: bfloat16 [4, 16384, 1024], P('pipe', 'dp'), may hold values from -6 to 6
- frozen_value_weight: bfloat16 [4, 8192, 1024], P('pipe'), may hold values from -0.1875 to 0.1875
- adapter_down_weight: bfloat16 [4, 128, 16, 8192], P('pipe', 'dp'), may hold values from -0.0625 to 0.0625
- adapter_up_weight: bfloat16 [4, 128, 16, 1024], P('pipe', 'dp'), may hold values from -0.1875 to 0.1875
- block_adapter_index: int32 [4, 128], P('pipe', 'dp'), may hold values from 0 to 63
- token_row_count: int32 [4, 128], P('pipe', 'dp'), may hold values from 32 to 128
- adapter_slot_table: int32 [64], replicated, may hold values from 0 to 63, as said below
Outputs:
- received: bfloat16 [4, 16384, 8192], P('pipe', 'dp')
- grad_a: bfloat16 [4, 64, 16, 8192], P('pipe', None, None, 'dp')
- grad_b: bfloat16 [4, 64, 16, 1024], P('pipe', None, None, 'dp')
The draws below stay inside these ranges and needn't reach their ends.
Inputs may be any that keep to these rules, and one draw needn't show every extreme that they name: adapter_slot_table is a permutation of 0 to 63.
All inputs are finite; a program needn't handle non-finite values.
Results may differ from the reference program's by a relative error of at most 0.0057.
Values may be sent and summed in bfloat16 or wider, within the bound.
No kernel may reach another device: no remote copies, remote signals or barrier semaphores. Data moves between devices by JAX's collectives and lax.ppermute only.
A program may use at most 128 MiB of HBM per device.

```python
import jax
import jax.numpy as jnp
from jax import lax

MODEL_WIDTH = 8192
VALUE_OUT_WIDTH = 1024
ADAPTER_RANK = 16
BLOCK_ROWS = 128
TOKENS = 16384
SECTION_BLOCKS = 128
ADAPTERS = 64
N_PIPE = 4


def draw_adapter_slot_table(key, part):
    key = jax.random.fold_in(key, 3)
    scores = jax.random.randint(key, (ADAPTERS,), 0, 4096) * ADAPTERS + jnp.arange(ADAPTERS, dtype=jnp.int32)
    return jnp.argsort(scores).astype(jnp.int32)


def set_ends(array, rng, low, largest):
    longest = array.shape.index(max(array.shape))
    spots = []
    for shift in (0, 1):
        where = [jax.random.randint(jax.random.fold_in(rng, axis), (), 0, length) for axis, length in enumerate(array.shape)]
        where[longest] = (where[longest] + shift) % array.shape[longest]
        spots.append(tuple(where))
    return array.at[spots[0]].set(low).at[spots[1]].set(largest)


def steps_of(own_key, extent, pieces, low, top_value):
    loudness = 1.0
    for position, shards_of in pieces:
        draws = jax.random.uniform(jax.random.fold_in(jax.random.fold_in(own_key, 6), position), (shards_of,), jnp.float32, low / len(pieces), top_value / len(pieces))
        loudness = loudness * jnp.repeat(jnp.exp(draws), extent[position] // shards_of).reshape((-1,) + (1,) * (len(extent) - 1 - position))
    return loudness


def gaussian(rng, dims, width, most, pieces=(), kind=jnp.bfloat16):
    drawn = jax.random.normal(rng, dims, jnp.float32) * width
    if len(pieces) > 0:
        drawn = steps_of(rng, dims, pieces, -0.22, 0.18) * drawn
    return jnp.clip(drawn, min=-most, max=most).astype(kind)


def setup_inputs(seed: int = 0) -> dict:
    key_of = jax.random.split(jax.random.key(seed), 9)
    acts = gaussian(key_of[0], (N_PIPE, TOKENS, MODEL_WIDTH), 1.0, 6.0, ((0, 4), (1, 32)))
    output_gradient = gaussian(key_of[1], (N_PIPE, TOKENS, VALUE_OUT_WIDTH), 1.0, 6.0, ((0, 4), (1, 32)))
    frozen_value_weight = gaussian(key_of[2], (N_PIPE, MODEL_WIDTH, VALUE_OUT_WIDTH), VALUE_OUT_WIDTH ** -0.5, 0.1875, ((0, 4),))
    adapter_down_weight = gaussian(key_of[3], (N_PIPE, SECTION_BLOCKS, ADAPTER_RANK, MODEL_WIDTH), MODEL_WIDTH ** -0.5, 0.0625, ((0, 4), (1, 32)))
    adapter_up_weight = gaussian(key_of[4], (N_PIPE, SECTION_BLOCKS, ADAPTER_RANK, VALUE_OUT_WIDTH), VALUE_OUT_WIDTH ** -0.5, 0.1875, ((0, 4), (1, 32)))
    block_adapter_index = set_ends(jax.random.randint(key_of[5], (N_PIPE, SECTION_BLOCKS), 0, ADAPTERS), jax.random.fold_in(key_of[5], 1), 0, ADAPTERS - 1).astype(jnp.int32)
    token_row_count = set_ends(jax.random.randint(key_of[6], (N_PIPE, SECTION_BLOCKS), 32, 129), jax.random.fold_in(key_of[6], 1), 32, 128).astype(jnp.int32)
    adapter_slot_table = draw_adapter_slot_table(jax.random.fold_in(key_of[8], 71), 0)
    return dict(acts=acts, output_gradient=output_gradient, frozen_value_weight=frozen_value_weight, adapter_down_weight=adapter_down_weight, adapter_up_weight=adapter_up_weight, block_adapter_index=block_adapter_index, token_row_count=token_row_count, adapter_slot_table=adapter_slot_table)


adapter_scale = 2.0


def section_backward(inputs, upstream, weight, down_matrix, up_matrix, live):
    live_count = live.shape[0]
    activation_rows = inputs.reshape(live_count, BLOCK_ROWS, MODEL_WIDTH)
    grad_rows = upstream.reshape(live_count, BLOCK_ROWS, VALUE_OUT_WIDTH)
    keep = jnp.arange(BLOCK_ROWS, dtype=jnp.int32)[None, :] < live[:, None]
    grad_rows = jnp.where(keep[:, :, None], grad_rows, jnp.zeros_like(grad_rows))
    activations_wide = activation_rows.astype(jnp.float32)
    gradient_wide = grad_rows.astype(jnp.float32)
    down_matrix_wide = down_matrix.astype(jnp.float32)
    up_matrix_wide = up_matrix.astype(jnp.float32)
    rank_activation = jnp.einsum("jug,jpg->jup", activations_wide, down_matrix_wide).astype(jnp.bfloat16)
    rank_gradient = (adapter_scale * jnp.einsum("mig,mjg->mij", gradient_wide, up_matrix_wide)).astype(jnp.bfloat16)
    down_gradient_part = jnp.einsum("sze,szv->sev", rank_gradient.astype(jnp.float32), activations_wide).astype(jnp.bfloat16)
    up_gradient_part = (adapter_scale * jnp.einsum("upg,upf->ugf", rank_activation.astype(jnp.float32), gradient_wide)).astype(jnp.bfloat16)
    base_term = lax.dot_general(grad_rows.reshape(live_count * BLOCK_ROWS, VALUE_OUT_WIDTH), weight,
                                (((1,), (1,)), ((), ())), preferred_element_type=jnp.float32)
    adapter_term = jnp.einsum("cyl,clp->cyp", rank_gradient.astype(jnp.float32), down_matrix_wide).reshape(live_count * BLOCK_ROWS, MODEL_WIDTH)
    return (base_term + adapter_term).astype(jnp.bfloat16), down_gradient_part, up_gradient_part


def reference(acts, output_gradient, frozen_value_weight, adapter_down_weight, adapter_up_weight, block_adapter_index, token_row_count, adapter_slot_table):
    passed_list = []
    grads_a = []
    grads_b = []
    for section_index in range(N_PIPE):
        passed, down_gradient_part, up_gradient_part = section_backward(acts[section_index], output_gradient[section_index], frozen_value_weight[section_index],
                                                  adapter_down_weight[section_index], adapter_up_weight[section_index], token_row_count[section_index])
        slot_of = adapter_slot_table[block_adapter_index[section_index]].astype(jnp.int32)
        total_a = jnp.zeros((ADAPTERS, ADAPTER_RANK, MODEL_WIDTH), jnp.float32).at[slot_of].add(down_gradient_part.astype(jnp.float32))
        total_b = jnp.zeros((ADAPTERS, ADAPTER_RANK, VALUE_OUT_WIDTH), jnp.float32).at[slot_of].add(up_gradient_part.astype(jnp.float32))
        passed_list.append(passed)
        grads_a.append(total_a.astype(jnp.bfloat16))
        grads_b.append(total_b.astype(jnp.bfloat16))
    shifted = passed_list[1:] + [jnp.zeros((TOKENS, MODEL_WIDTH), jnp.bfloat16)]
    return jnp.stack(shifted), jnp.stack(grads_a), jnp.stack(grads_b)
```

```python
import functools

import jax
import jax.numpy as jnp
from jax import lax
from jax.experimental import pallas as pl
from jax.experimental.pallas import tpu as pltpu
from jax.sharding import PartitionSpec as P

BLOCK_ROWS = 128
RANK = 16
BF16 = jnp.bfloat16
F32 = jnp.float32

adapter_scale = 2.0

LAST = (((1,), (1,)), ((), ()))
FIRST = (((0,), (0,)), ((), ()))


def dot(a, b, dims=(((1,), (0,)), ((), ()))):
    return lax.dot_general(a, b, dims, preferred_element_type=F32)


def vmem(mib):
    return pltpu.CompilerParams(vmem_limit_bytes=mib << 20)


def prepare_kernel(count_ref, grad_ref, up_ref, message_ref):
    blocks = count_ref.shape[0]
    rows, width = grad_ref.shape
    message_ref[rows:, :] = jnp.zeros((RANK, width), BF16)
    for b in range(blocks):
        span = slice(b * BLOCK_ROWS, (b + 1) * BLOCK_ROWS)
        at = lax.broadcasted_iota(jnp.int32, (BLOCK_ROWS, width), 0)
        masked = jnp.where(at < count_ref[b], grad_ref[span, :].astype(F32), 0.0).astype(BF16)
        message_ref[span, :] = masked
        low = dot(up_ref[b * RANK : (b + 1) * RANK, :], masked, LAST)
        message_ref[rows:, span] = (adapter_scale * low).astype(BF16)


def prepare(count, grad, up):
    rows, width = grad.shape
    return pl.pallas_call(
        prepare_kernel,
        out_shape=jax.ShapeDtypeStruct((rows + RANK, width), BF16),
        in_specs=[
            pl.BlockSpec(memory_space=pltpu.SMEM),
            pl.BlockSpec(memory_space=pltpu.VMEM),
            pl.BlockSpec(memory_space=pltpu.VMEM),
        ],
        out_specs=pl.BlockSpec(memory_space=pltpu.VMEM),
        compiler_params=vmem(24),
        name="prepare",
    )(count, grad, up)


def grads_kernel(groups, ids_ref, table_ref, message_ref, acts_ref, down_ref, out_ref, low_ref):
    step = pl.program_id(0)
    blocks = ids_ref.shape[0]
    rows, chunk = acts_ref.shape
    take = out_ref.shape[2]

    @pl.when(step == 0)
    def _():
        low_ref[...] = jnp.zeros_like(low_ref)

    for b in range(blocks):
        span = slice(b * BLOCK_ROWS, (b + 1) * BLOCK_ROWS)
        ranks = slice(b * RANK, (b + 1) * RANK)
        acts = acts_ref[span, :]
        low_ref[ranks, :] += dot(down_ref[ranks, :], acts, LAST)
        part = dot(message_ref[rows:, span], acts).astype(BF16)
        for k in range(chunk // take):
            out_ref[step * (chunk // take) + k, ranks, :] = part[:, k * take : (k + 1) * take]

    @pl.when(step == pl.num_programs(0) - 1)
    def _():
        parts = []
        for b in range(blocks):
            span = slice(b * BLOCK_ROWS, (b + 1) * BLOCK_ROWS)
            low = low_ref[b * RANK : (b + 1) * RANK, :].astype(BF16)
            parts.append(adapter_scale * dot(low, message_ref[span, :]))
        part = jnp.concatenate(parts, axis=0)
        width = part.shape[1] // groups
        lane = lax.broadcasted_iota(jnp.int32, (8, 128), 1) // width
        row = lax.broadcasted_iota(jnp.int32, (8, take), 0)
        slots = jnp.zeros((8, take), F32)
        for b in range(blocks):
            slots = jnp.where(row == b, table_ref[ids_ref[b]].astype(F32), slots)
        fit = 128 // width
        for d in range(groups):
            column, mine = d // fit, d % fit
            halves = []
            for h in range(take // 128):
                total = jnp.zeros((8, 128), F32)
                for g in range(fit):
                    k = h * fit + g
                    tile = part[8 * k : 8 * k + 8, 128 * column : 128 * column + 128]
                    tile = pltpu.roll(tile, ((g - mine) * width) % 128, 1)
                    total = jnp.where(lane == g, tile, total)
                halves.append(total)
            packed = jnp.concatenate([jnp.concatenate(halves, axis=1), slots], axis=0)
            out_ref[d, blocks * RANK :, :] = packed.astype(BF16)


def grads(ids, table, message, acts, down, groups):
    blocks = ids.shape[0]
    rows, width = acts.shape
    chunk = 1024
    shape = (groups, blocks * RANK + 16, width // groups)
    return pl.pallas_call(
        functools.partial(grads_kernel, groups),
        out_shape=jax.ShapeDtypeStruct(shape, BF16),
        grid=(width // chunk,),
        in_specs=[
            pl.BlockSpec(memory_space=pltpu.SMEM),
            pl.BlockSpec(memory_space=pltpu.SMEM),
            pl.BlockSpec(message.shape, lambda i: (0, 0)),
            pl.BlockSpec((rows, chunk), lambda i: (0, i)),
            pl.BlockSpec((blocks * RANK, chunk), lambda i: (0, i)),
        ],
        out_specs=pl.BlockSpec(shape, lambda i: (0, 0, 0)),
        scratch_shapes=[pltpu.VMEM((blocks * RANK, BLOCK_ROWS), F32)],
        compiler_params=vmem(32),
        name="grads",
    )(ids, table, message, acts, down)


def product_kernel(message_ref, weight_ref, down_ref, out_ref):
    rows = out_ref.shape[0]
    ranks = down_ref.shape[0]
    low = jnp.concatenate([message_ref[rows:, :rows].astype(F32)] * (ranks // RANK), axis=0)
    own = lax.broadcasted_iota(jnp.int32, low.shape, 0) // RANK
    of = lax.broadcasted_iota(jnp.int32, low.shape, 1) // BLOCK_ROWS
    low = jnp.where(own == of, low, 0.0).astype(BF16)
    total = dot(message_ref[:rows, :], weight_ref[...], LAST) + dot(low, down_ref[...], FIRST)
    out_ref[...] = total.astype(BF16)


def product(message, weight, down):
    width, depth = weight.shape
    rows = message.shape[0] - RANK
    chunk = 1024
    return pl.pallas_call(
        product_kernel,
        out_shape=jax.ShapeDtypeStruct((rows, width), BF16),
        grid=(width // chunk,),
        in_specs=[
            pl.BlockSpec(message.shape, lambda i: (0, 0)),
            pl.BlockSpec((chunk, depth), lambda i: (i, 0)),
            pl.BlockSpec((down.shape[0], chunk), lambda i: (0, i)),
        ],
        out_specs=pl.BlockSpec((rows, chunk), lambda i: (0, i)),
        compiler_params=vmem(40),
        name="product",
    )(message, weight, down)


def body(
    acts,
    output_gradient,
    frozen_value_weight,
    adapter_down_weight,
    adapter_up_weight,
    block_adapter_index,
    token_row_count,
    adapter_slot_table,
):
    blocks = token_row_count.shape[1]
    rows, width = acts.shape[1:]
    depth = output_gradient.shape[2]
    adapters = adapter_slot_table.shape[0]
    groups = lax.axis_size("dp")
    down = adapter_down_weight.reshape(blocks * RANK, width)
    up = adapter_up_weight.reshape(blocks * RANK, depth)

    def back(x):
        n = lax.axis_size("pipe")
        return lax.ppermute(x, "pipe", [(i + 1, i) for i in range(n - 1)])

    share = lax.dynamic_slice_in_dim(
        frozen_value_weight[0], lax.axis_index("dp") * (width // groups), width // groups, 0
    )
    share = back(share)
    message = prepare(token_row_count[0], output_gradient[0], up)
    send = grads(block_adapter_index[0], adapter_slot_table, message, acts[0], down, groups)
    weight = lax.all_gather(share, "dp", axis=0, tiled=True)
    got = lax.all_to_all(send, "dp", split_axis=0, concat_axis=0, tiled=True)
    message, down, share = lax.optimization_barrier((message, down, share))
    message, down = back(message), back(down)
    received = product(message, weight, down)

    ranks = blocks * RANK
    slot = got[:, ranks + 8 : ranks + 8 + blocks, 0].reshape(-1)
    pick = (jnp.arange(adapters, dtype=BF16)[:, None] == slot[None, :]).astype(BF16)
    terms = got[:, :ranks, :].reshape(groups * blocks, RANK, width // groups)
    total_a = jnp.einsum("js,srd->jrd", pick, terms, preferred_element_type=F32)
    terms = got[:, ranks : ranks + 8, :].reshape(groups, 8, ranks // 8, depth // groups)
    terms = jnp.swapaxes(terms, 1, 2).reshape(groups * blocks, RANK, depth // groups)
    total_b = jnp.einsum("js,srd->jrd", pick, terms, preferred_element_type=F32)
    return received[None], total_a.astype(BF16)[None], total_b.astype(BF16)[None]


def solution(mesh):
    in_specs = (
        P("pipe", "dp", None),
        P("pipe", "dp", None),
        P("pipe", None, None),
        P("pipe", "dp", None, None),
        P("pipe", "dp", None, None),
        P("pipe", "dp"),
        P("pipe", "dp"),
        P(),
    )
    out_specs = (P("pipe", "dp", None), P("pipe", None, None, "dp"), P("pipe", None, None, "dp"))
    return jax.shard_map(body, mesh=mesh, in_specs=in_specs, out_specs=out_specs, check_vma=False)
```

```python
import functools

import jax
import jax.numpy as jnp
from jax import lax
from jax.experimental import pallas as pl
from jax.experimental.pallas import tpu as pltpu
from jax.sharding import PartitionSpec as P

BLOCK_ROWS = 128
RANK = 16
BF16 = jnp.bfloat16
F32 = jnp.float32

adapter_scale = 2.0

SIDE, CORES = 4, 2
PIECE = 128
BLOCK = SIDE * PIECE
EARLY = 384
HBM = pltpu.MemorySpace.HBM

LAST = (((1,), (1,)), ((), ()))
FIRST = (((0,), (0,)), ((), ()))


def dot(a, b, dims=(((1,), (0,)), ((), ()))):
    return lax.dot_general(a, b, dims, preferred_element_type=F32)


def vmem(mib):
    return pltpu.CompilerParams(vmem_limit_bytes=mib << 20)


def in_hbm(*arrays):
    return [pltpu.with_memory_space_constraint(a, HBM) for a in arrays]


def front_kernel(count_h, grad_ref, up_ref, acts_ref, down_ref, early_ref, late_ref, low_ref,
                 send_ref, count_ref, grad_v, up_v, acts_v, down_v, low_v, message_v,
                 send_v, in_sems, acts_sems, down_sems, out_sems, down_out_sems):
    blocks = count_ref.shape[1]
    rows, depth = grad_v.shape
    chunks, _, wide = acts_v.shape
    take = send_v.shape[2]
    ranks = blocks * RANK
    grad_in = pltpu.make_async_copy(grad_ref, grad_v, in_sems.at[0])
    up_in = pltpu.make_async_copy(up_ref, up_v, in_sems.at[1])
    count_in = pltpu.make_async_copy(count_h, count_ref, in_sems.at[2])
    count_in.start()
    grad_in.start()
    up_in.start()
    acts_in, down_in = [], []
    for i in range(chunks):
        span = pl.ds(i * wide, wide)
        acts_in.append(pltpu.make_async_copy(acts_ref.at[:, span], acts_v.at[i], acts_sems.at[i]))
        down_in.append(pltpu.make_async_copy(down_ref.at[:, span], down_v.at[i], down_sems.at[i]))
        down_in[i].start()
        acts_in[i].start()
    message_v[rows:, :] = jnp.zeros((RANK, depth), BF16)
    count_in.wait()
    grad_in.wait()
    up_in.wait()
    for b in range(blocks):
        span = slice(b * BLOCK_ROWS, (b + 1) * BLOCK_ROWS)
        at = lax.broadcasted_iota(jnp.int32, (BLOCK_ROWS, depth), 0)
        masked = jnp.where(at < count_ref[0, b], grad_v[span, :].astype(F32), 0.0).astype(BF16)
        message_v[span, :] = masked
        low = dot(up_v[b * RANK : (b + 1) * RANK, :], masked, LAST)
        message_v[rows:, span] = (adapter_scale * low).astype(BF16)
    rest = rows + RANK - EARLY
    outs = [
        pltpu.make_async_copy(message_v.at[pl.ds(0, EARLY)], early_ref, out_sems.at[0]),
        pltpu.make_async_copy(message_v.at[pl.ds(EARLY, rest)], late_ref.at[pl.ds(0, rest)], out_sems.at[1]),
    ]
    for out in outs:
        out.start()
    low_v[...] = jnp.zeros_like(low_v)
    fan = wide // take
    for i in range(chunks):
        acts_in[i].wait()
        down_in[i].wait()
        outs.append(pltpu.make_async_copy(
            down_v.at[i], late_ref.at[pl.ds(rest + i * ranks, ranks)], down_out_sems.at[i]
        ))
        outs[-1].start()
        for b in range(blocks):
            span = slice(b * BLOCK_ROWS, (b + 1) * BLOCK_ROWS)
            own = slice(b * RANK, (b + 1) * RANK)
            acts = acts_v[i, span, :]
            low_v[own, :] += dot(down_v[i, own, :], acts, LAST)
            part = dot(message_v[rows:, span], acts).astype(BF16)
            for k in range(fan):
                send_v[i * fan + k, own, :] = part[:, k * take : (k + 1) * take]
        there = (pl.ds(i * fan, fan), pl.ds(0, ranks))
        outs.append(pltpu.make_async_copy(send_v.at[there], send_ref.at[there], out_sems.at[2 + i]))
        outs[-1].start()
    low_ref[...] = low_v[...].astype(BF16)
    for out in outs:
        out.wait()


def front(count, grad, up, acts, down, groups):
    blocks = count.shape[1]
    rows, width = acts.shape
    depth = grad.shape[1]
    wide = depth
    chunks = width // wide
    ranks = blocks * RANK
    shape = jax.ShapeDtypeStruct
    hbm = pl.BlockSpec(memory_space=HBM)
    return pl.pallas_call(
        front_kernel,
        out_shape=(
            shape((EARLY, depth), BF16),
            shape((rows + RANK - EARLY + chunks * ranks, depth), BF16),
            shape((ranks, BLOCK_ROWS), BF16),
            shape((groups, ranks + 16, width // groups), BF16),
        ),
        in_specs=[hbm] * 5,
        out_specs=(hbm, hbm, pl.BlockSpec(memory_space=pltpu.VMEM), hbm),
        scratch_shapes=[
            pltpu.SMEM(count.shape, jnp.int32),
            pltpu.VMEM((rows, depth), BF16),
            pltpu.VMEM((ranks, depth), BF16),
            pltpu.VMEM((chunks, rows, wide), BF16),
            pltpu.VMEM((chunks, ranks, wide), BF16),
            pltpu.VMEM((ranks, BLOCK_ROWS), F32),
            pltpu.VMEM((rows + RANK, depth), BF16),
            pltpu.VMEM((groups, ranks, width // groups), BF16),
            pltpu.SemaphoreType.DMA((3,)),
            pltpu.SemaphoreType.DMA((chunks,)),
            pltpu.SemaphoreType.DMA((chunks,)),
            pltpu.SemaphoreType.DMA((chunks + 2,)),
            pltpu.SemaphoreType.DMA((chunks,)),
        ],
        compiler_params=vmem(16),
        cost_estimate=pl.CostEstimate(flops=10**10, transcendentals=0, bytes_accessed=3 * rows * width),
        name="front",
    )(*in_hbm(count, grad, up, acts, down))


def finish_kernel(ids_h, table_h, early_h, late_h, low_ref, send_in, send_ref, ids_ref, table_ref, message_v,
                  send_v, sems):
    blocks = ids_ref.shape[1]
    ranks = blocks * RANK
    rows, depth = message_v.shape
    groups, _, take = send_v.shape
    ins = [
        pltpu.make_async_copy(ids_h, ids_ref, sems.at[0]),
        pltpu.make_async_copy(table_h, table_ref, sems.at[1]),
        pltpu.make_async_copy(early_h, message_v.at[pl.ds(0, EARLY)], sems.at[2]),
        pltpu.make_async_copy(late_h.at[pl.ds(0, rows - EARLY)], message_v.at[pl.ds(EARLY, rows - EARLY)], sems.at[4]),
    ]
    for copy in ins:
        copy.start()
    for copy in ins:
        copy.wait()
    parts = []
    for b in range(blocks):
        span = slice(b * BLOCK_ROWS, (b + 1) * BLOCK_ROWS)
        low = low_ref[b * RANK : (b + 1) * RANK, :]
        parts.append(adapter_scale * dot(low, message_v[span, :]))
    part = jnp.concatenate(parts, axis=0)
    width = depth // groups
    lane = lax.broadcasted_iota(jnp.int32, (8, 128), 1) // width
    row = lax.broadcasted_iota(jnp.int32, (8, take), 0)
    turn = lax.broadcasted_iota(jnp.int32, (8, take), 1) // RANK % blocks
    slots = jnp.zeros((8, take), F32)
    for b in range(blocks):
        here = ((row == 0) & (turn == b)) | (row == 1 + b)
        slots = jnp.where(here, table_ref[ids_ref[0, b]].astype(F32), slots)
    fit = 128 // width
    for d in range(groups):
        column, mine = d // fit, d % fit
        halves = []
        for h in range(take // 128):
            total = jnp.zeros((8, 128), F32)
            for g in range(fit):
                k = h * fit + g
                tile = part[8 * k : 8 * k + 8, 128 * column : 128 * column + 128]
                tile = pltpu.roll(tile, ((g - mine) * width) % 128, 1)
                total = jnp.where(lane == g, tile, total)
            halves.append(total)
        packed = jnp.concatenate([jnp.concatenate(halves, axis=1), slots], axis=0)
        send_v[d] = packed.astype(BF16)
    out = pltpu.make_async_copy(send_v, send_ref.at[pl.ds(0, groups), pl.ds(ranks, 16)], sems.at[3])
    out.start()
    out.wait()


def finish(ids, table, early, late, low, send):
    hbm = pl.BlockSpec(memory_space=HBM)
    groups, _, take = send.shape
    rows, depth = ids.shape[1] * BLOCK_ROWS, early.shape[1]
    return pl.pallas_call(
        finish_kernel,
        out_shape=jax.ShapeDtypeStruct(send.shape, BF16),
        in_specs=[hbm] * 4 + [pl.BlockSpec(memory_space=pltpu.VMEM), hbm],
        out_specs=hbm,
        scratch_shapes=[
            pltpu.SMEM(ids.shape, jnp.int32),
            pltpu.SMEM(table.shape, jnp.int32),
            pltpu.VMEM((rows, depth), BF16),
            pltpu.VMEM((groups, 16, take), BF16),
            pltpu.SemaphoreType.DMA((5,)),
        ],
        input_output_aliases={5: 0},
        compiler_params=vmem(8),
        cost_estimate=pl.CostEstimate(flops=2 * 10**9, transcendentals=0, bytes_accessed=2 * rows * depth),
        name="finish",
    )(*in_hbm(ids, table, early, late), low, *in_hbm(send))


def join_kernel(counts, spots_ref, *refs):
    parts, outs = refs[: sum(counts)], refs[sum(counts) :]
    i = 0
    for n, out in zip(counts, outs):
        rows = parts[i].shape[0]
        for part in parts[i : i + n]:
            at = pl.multiple_of(spots_ref[i] * rows, rows)
            out[pl.ds(at, rows), :] = part[...]
            i += 1


def join(spots, *groups, cost):
    counts = tuple(len(g) for g in groups)
    in_vmem = pl.BlockSpec(memory_space=pltpu.VMEM)
    return pl.pallas_call(
        functools.partial(join_kernel, counts),
        out_shape=[jax.ShapeDtypeStruct((sum(v.shape[0] for v in g), g[0].shape[1]), BF16) for g in groups],
        in_specs=[pl.BlockSpec(memory_space=pltpu.SMEM)] + [in_vmem] * sum(counts),
        out_specs=[in_vmem] * len(groups),
        compiler_params=vmem(4),
        cost_estimate=pl.CostEstimate(flops=cost, transcendentals=0, bytes_accessed=1 << 21),
        name="join",
    )(spots, *[v for g in groups for v in g])


def collect_kernel(got_h, out_a, out_b, a_v, tail_v, pick_v, sems):
    sources, ranks, take = a_v.shape
    adapters = out_a.shape[0]
    blocks = ranks // RANK
    ins = [
        pltpu.make_async_copy(got_h.at[pl.ds(0, sources), pl.ds(ranks, 16)], tail_v, sems.at[0]),
        pltpu.make_async_copy(got_h.at[pl.ds(0, sources), pl.ds(0, ranks)], a_v, sems.at[1]),
    ]
    for copy in ins:
        copy.start()
    ins[0].wait()
    tail = tail_v[...].astype(F32)
    lane = lax.broadcasted_iota(jnp.int32, (RANK, 128), 1)
    same = lane % RANK == lax.broadcasted_iota(jnp.int32, (RANK, 128), 0)
    fit = 128 // ranks
    for v in range(sources // fit):
        slots = jnp.broadcast_to(tail[v * fit, 8:9, :128], (RANK, 128))
        for k in range(1, fit):
            row = jnp.broadcast_to(tail[v * fit + k, 8:9, :128], (RANK, 128))
            slots = jnp.where(lane // ranks == k, row, slots)
        slots = jnp.where(same, slots, -1.0)
        for j in range(adapters):
            pick = jnp.where(slots == float(j), 1.0, 0.0).astype(BF16)
            pick_v[j * RANK : (j + 1) * RANK, v * 128 : (v + 1) * 128] = pick
    ins[1].wait()
    total = dot(pick_v[...], a_v[...].reshape(sources * ranks, take))
    out_a[...] = total.reshape(adapters, RANK, take).astype(BF16)

    width = out_b.shape[1]
    terms = tail[:, :8, :].reshape(sources * 8, take).astype(BF16)
    lane = lax.broadcasted_iota(jnp.int32, (adapters, sources * 8), 1)
    slot = lax.broadcasted_iota(jnp.int32, (adapters, sources * 8), 0).astype(F32)
    sums = []
    for b in range(blocks):
        slots = jnp.zeros((1, sources * 8), F32)
        for source in range(sources):
            slots = jnp.where(lane[:1] // 8 == source, tail[source, 9 + b : 10 + b, : sources * 8], slots)
        hit = slots == slot
        pick = jnp.concatenate([jnp.where(hit & (lane % 8 == r), 1.0, 0.0) for r in range(8)], axis=0)
        at = b * 2 * width
        total = dot(pick.astype(BF16), terms[:, at // 128 * 128 : at // 128 * 128 + 128])
        sums.append(pltpu.roll(total, (128 - at % 128) % 128, 1))
    total = sums[0]
    for more in sums[1:]:
        total = total + more
    for r in range(8):
        turned = total[r * adapters : (r + 1) * adapters, :].T
        out_b[r] = turned[:width].astype(BF16)
        out_b[8 + r] = turned[width : 2 * width].astype(BF16)


def collect(got, adapters, blocks, depth):
    groups, _, take = got.shape
    ranks = blocks * RANK
    in_vmem = pl.BlockSpec(memory_space=pltpu.VMEM)
    return pl.pallas_call(
        collect_kernel,
        out_shape=(
            jax.ShapeDtypeStruct((adapters, RANK, take), BF16),
            jax.ShapeDtypeStruct((RANK, depth // groups, adapters), BF16),
        ),
        in_specs=[pl.BlockSpec(memory_space=HBM)],
        out_specs=(in_vmem, in_vmem),
        scratch_shapes=[
            pltpu.VMEM((groups, ranks, take), BF16),
            pltpu.VMEM((groups, 16, take), BF16),
            pltpu.VMEM((adapters * RANK, groups * ranks), BF16),
            pltpu.SemaphoreType.DMA((2,)),
        ],
        compiler_params=vmem(20),
        cost_estimate=pl.CostEstimate(flops=4 * 10**9, transcendentals=0, bytes_accessed=4 * got.size),
        name="collect",
    )(*in_hbm(got))


def unpack_kernel(early_ref, late_ref, message_ref, low_ref, down_ref):
    rows = message_ref.shape[0]
    ranks = low_ref.shape[1]
    rest = rows - EARLY
    message_ref[:EARLY, :] = early_ref[...]
    message_ref[EARLY:, :] = late_ref[:rest, :]
    down_ref[...] = late_ref[rest + RANK :, :]
    low = jnp.concatenate([late_ref[rest : rest + RANK, :rows].astype(F32)] * (ranks // RANK), axis=0)
    own = lax.broadcasted_iota(jnp.int32, low.shape, 0) // RANK
    of = lax.broadcasted_iota(jnp.int32, low.shape, 1) // BLOCK_ROWS
    low_ref[...] = jnp.where(own == of, low, 0.0).T.astype(BF16)


def unpack(early, late, rows, ranks):
    depth = early.shape[1]
    shape = jax.ShapeDtypeStruct
    in_vmem = pl.BlockSpec(memory_space=pltpu.VMEM)
    return pl.pallas_call(
        unpack_kernel,
        out_shape=(
            shape((rows, depth), BF16),
            shape((rows, ranks), BF16),
            shape((late.shape[0] + EARLY - rows - RANK, depth), BF16),
        ),
        in_specs=[in_vmem] * 2,
        out_specs=(in_vmem,) * 3,
        compiler_params=vmem(4),
        name="unpack",
    )(early, late)


def product_kernel(which, alias, starts_ref, message_ref, low_ref, down_ref, *refs):
    n = len(which)
    blocks = refs[:n]
    out_ref, out_v, out_sems = refs[n + alias :]
    ranks, wide = low_ref.shape[1], down_ref.shape[1]
    outs = []
    for i in range(n):
        start = pl.multiple_of(starts_ref[which[i]], BLOCK)
        chunk = pl.ds(pl.multiple_of(start // wide * ranks, ranks), ranks)
        down = down_ref[chunk, pl.ds(pl.multiple_of(start % wide, BLOCK), BLOCK)]
        total = dot(message_ref[...], blocks[i][...], LAST) + dot(low_ref[...], down)
        out_v[i] = total.astype(BF16)
        out = pltpu.make_async_copy(out_v.at[i], out_ref.at[:, pl.ds(start, BLOCK)], out_sems.at[i])
        out.start()
        outs.append(out)
    for out in outs:
        out.wait()


def product(blocks, starts, message, low, down, before, name):
    n = len(blocks)
    rows, depth = message.shape
    width = down.size // low.shape[1]
    operands = [starts, message, low, down, *[b[0] for b in blocks]]
    in_vmem = pl.BlockSpec(memory_space=pltpu.VMEM)
    in_specs = [pl.BlockSpec(memory_space=pltpu.SMEM)] + [in_vmem] * (len(operands) - 1)
    hbm = pl.BlockSpec(memory_space=HBM)
    if before is not None:
        operands += in_hbm(before)
        in_specs.append(hbm)
    columns = n * BLOCK
    return pl.pallas_call(
        functools.partial(product_kernel, tuple(b[1] for b in blocks), before is not None),
        out_shape=jax.ShapeDtypeStruct((rows, width), BF16),
        in_specs=in_specs,
        out_specs=hbm,
        scratch_shapes=[pltpu.VMEM((n, rows, BLOCK), BF16), pltpu.SemaphoreType.DMA((n,))],
        input_output_aliases={} if before is None else {len(operands) - 1: 0},
        compiler_params=vmem(12),
        cost_estimate=pl.CostEstimate(
            flops=3 * rows * depth * columns, transcendentals=0, bytes_accessed=2 * columns * (depth + rows)
        ),
        name=name,
    )(*operands)


def spot(at, core):
    return (at + core) % SIDE


def near(at, core):
    return ((spot(at, core) ^ 1) - core) % SIDE


def far(at, core):
    return (SIDE - 1 - spot(at, core) - core) % SIDE


def moved(array, to):
    route = []
    for d in range(SIDE * SIDE * CORES):
        x, z, core = to(d // (SIDE * CORES), d // CORES % SIDE, d % CORES)
        route.append((d, (x * SIDE + z) * CORES + core))
    return lax.ppermute(array, "dp", route)


def x_near(x, z, core):
    return near(x, core), z, core


def x_far(x, z, core):
    return far(x, core), z, core


def z_near(x, z, core):
    return x, near(z, core), core


def z_far(x, z, core):
    return x, far(z, core), core


def other_core(x, z, core):
    return x, z, 1 - core


def places(line, core):
    steps = (line, near(line, core), far(line, core), near(far(line, core), core))
    return [(s * CORES + core) * BLOCK for s in steps]


def hop(x, route):
    return lax.ppermute(x, "pipe", route)


def tie(*arrays):
    return lax.optimization_barrier(arrays)


def body(
    acts,
    output_gradient,
    frozen_value_weight,
    adapter_down_weight,
    adapter_up_weight,
    block_adapter_index,
    token_row_count,
    adapter_slot_table,
):
    blocks = token_row_count.shape[1]
    rows, width = acts.shape[1:]
    depth = output_gradient.shape[2]
    adapters = adapter_slot_table.shape[0]
    groups = lax.axis_size("dp")
    down = adapter_down_weight.reshape(blocks * RANK, width)
    up = adapter_up_weight.reshape(blocks * RANK, depth)
    half = width // 2
    me = lax.axis_index("dp")
    x, z, core = me // (SIDE * CORES), me // CORES % SIDE, me % CORES
    back = [(1, 0), (2, 1), (3, 2)]

    piece_a = lax.dynamic_slice_in_dim(
        frozen_value_weight[0], ((z * CORES + core) * SIDE + spot(x, core)) * PIECE, PIECE, 0
    )
    piece_b = lax.dynamic_slice_in_dim(
        frozen_value_weight[0], half + ((x * CORES + core) * SIDE + spot(z, core)) * PIECE, PIECE, 0
    )
    a0, b0 = hop(piece_a, back), hop(piece_b, back)
    early, late, low, send = front(token_row_count, output_gradient[0], up, acts[0], down, groups)
    spot_a, spot_b = spot(x, core), spot(z, core)
    halves = jnp.stack([spot_a % 2, 1 - spot_a % 2, spot_b % 2, 1 - spot_b % 2]).astype(jnp.int32)
    wholes = jnp.stack([spot_a // 2, 1 - spot_a // 2, spot_b // 2, 1 - spot_b // 2]).astype(jnp.int32)
    starts = []
    for c in (core, 1 - core):
        starts += places(z, c) + [half + s for s in places(x, c)]
    starts = jnp.stack(starts).astype(jnp.int32)
    a0, b0, send, early, late, low, halves, wholes, starts = tie(
        a0, b0, send, early, late, low, halves, wholes, starts
    )

    a1, b1 = moved(a0, x_near), moved(b0, z_near)
    send = finish(block_adapter_index, adapter_slot_table, early, late, low, send)
    early = hop(early, back)
    got = lax.all_to_all(send, "dp", split_axis=0, concat_axis=0, tiled=True)
    a0, b0, a1, b1, send, late = tie(a0, b0, a1, b1, send, late)

    ap, bp = join(halves, (a0, a1), (b0, b1), cost=10**6)
    aq, bq = moved(ap, x_far), moved(bp, z_far)
    aq, bq, ap, bp, early, late = tie(aq, bq, ap, bp, early, late)

    late = hop(late, back)
    a, b = join(wholes, (ap, aq), (bp, bq), cost=10**6)
    a_near, b_near = moved(a, z_near), moved(b, x_near)
    a_far, b_far = moved(a, z_far), moved(b, x_far)
    total_a, total_b = collect(got, adapters, blocks, depth)
    a, b, a_near, b_near, a_far, b_far, late, total_a, total_b = tie(
        a, b, a_near, b_near, a_far, b_far, late, total_a, total_b
    )

    def pair(a, b, step, mine=True):
        at = step if mine else step + 2 * SIDE
        return [(a, at), (b, at + SIDE)]

    def others(a, b, step):
        return pair(moved(a, other_core), moved(b, other_core), step, False)

    a_last, b_last = moved(a_near, z_far), moved(b_near, x_far)
    shared = (starts, *unpack(early, late, rows, blocks * RANK))
    mine = pair(a, b, 0) + pair(a_near, b_near, 1) + pair(a_far, b_far, 2)
    theirs = others(a, b, 0) + others(a_near, b_near, 1) + others(a_far, b_far, 2)
    received = product(mine, *shared, None, "product_mine")
    received = product(theirs, *shared, received, "product_theirs")
    received, a_last, b_last = tie(received, a_last, b_last)
    theirs = others(a_last, b_last, 3)
    received = product(pair(a_last, b_last, 3), *shared, received, "product_last")
    received = product(theirs, *shared, received, "product_end")
    return received[None], total_a[None], jnp.transpose(total_b, (2, 0, 1))[None]


def solution(mesh):
    in_specs = (
        P("pipe", "dp", None),
        P("pipe", "dp", None),
        P("pipe", None, None),
        P("pipe", "dp", None, None),
        P("pipe", "dp", None, None),
        P("pipe", "dp"),
        P("pipe", "dp"),
        P(),
    )
    out_specs = (P("pipe", "dp", None), P("pipe", None, None, "dp"), P("pipe", None, None, "dp"))
    return jax.shard_map(body, mesh=mesh, in_specs=in_specs, out_specs=out_specs, check_vma=False)
```

```python
import functools

import jax
import jax.numpy as jnp
from jax import lax
from jax.experimental import pallas as pl
from jax.experimental.pallas import tpu as pltpu
from jax.sharding import PartitionSpec as P

BLOCK_ROWS = 128
RANK = 16
BF16 = jnp.bfloat16
F32 = jnp.float32

adapter_scale = 2.0

SIDE, CORES = 4, 2
PIECE = 128
BLOCK = SIDE * PIECE
EARLY = 320
HBM = pltpu.MemorySpace.HBM

LAST = (((1,), (1,)), ((), ()))
FIRST = (((0,), (0,)), ((), ()))


def dot(a, b, dims=(((1,), (0,)), ((), ()))):
    return lax.dot_general(a, b, dims, preferred_element_type=F32)


def vmem(mib):
    return pltpu.CompilerParams(vmem_limit_bytes=mib << 20)


def in_hbm(*arrays):
    return [pltpu.with_memory_space_constraint(a, HBM) for a in arrays]


def front_kernel(count_h, ids_h, table_h, grad_ref, up_ref, acts_ref, down_ref, early_ref, late_ref,
                 send_ref, count_ref, ids_ref, table_ref, grad_v, up_v, acts_v, down_v, low_v,
                 message_v, send_v, in_sems, acts_sems, down_sems, out_sems, down_out_sems):
    blocks = count_ref.shape[1]
    rows, depth = grad_v.shape
    chunks, _, wide = acts_v.shape
    groups, _, take = send_v.shape
    ranks = blocks * RANK
    ins = [
        pltpu.make_async_copy(count_h, count_ref, in_sems.at[0]),
        pltpu.make_async_copy(grad_ref, grad_v, in_sems.at[1]),
        pltpu.make_async_copy(up_ref, up_v, in_sems.at[2]),
        pltpu.make_async_copy(ids_h, ids_ref, in_sems.at[3]),
        pltpu.make_async_copy(table_h, table_ref, in_sems.at[4]),
    ]
    for copy in ins:
        copy.start()
    acts_in, down_in = [], []
    for i in range(chunks):
        span = pl.ds(i * wide, wide)
        acts_in.append(pltpu.make_async_copy(acts_ref.at[:, span], acts_v.at[i], acts_sems.at[i]))
        down_in.append(pltpu.make_async_copy(down_ref.at[:, span], down_v.at[i], down_sems.at[i]))
        down_in[i].start()
        acts_in[i].start()
    message_v[rows:, :] = jnp.zeros((RANK, depth), BF16)
    for copy in ins:
        copy.wait()
    for b in range(blocks):
        span = slice(b * BLOCK_ROWS, (b + 1) * BLOCK_ROWS)
        at = lax.broadcasted_iota(jnp.int32, (BLOCK_ROWS, depth), 0)
        masked = jnp.where(at < count_ref[0, b], grad_v[span, :].astype(F32), 0.0).astype(BF16)
        message_v[span, :] = masked
        low = dot(up_v[b * RANK : (b + 1) * RANK, :], masked, LAST)
        message_v[rows:, span] = (adapter_scale * low).astype(BF16)
    rest = rows + RANK - EARLY
    outs = [
        pltpu.make_async_copy(message_v.at[pl.ds(0, EARLY)], early_ref, out_sems.at[0]),
        pltpu.make_async_copy(message_v.at[pl.ds(EARLY, rest)], late_ref.at[pl.ds(0, rest)], out_sems.at[1]),
    ]
    for out in outs:
        out.start()
    low_v[...] = jnp.zeros_like(low_v)
    fan = wide // take
    for i in range(chunks):
        acts_in[i].wait()
        down_in[i].wait()
        outs.append(pltpu.make_async_copy(
            down_v.at[i], late_ref.at[pl.ds(rest + i * ranks, ranks)], down_out_sems.at[i]
        ))
        outs[-1].start()
        for b in range(blocks):
            span = slice(b * BLOCK_ROWS, (b + 1) * BLOCK_ROWS)
            own = slice(b * RANK, (b + 1) * RANK)
            acts = acts_v[i, span, :]
            low_v[own, :] += dot(down_v[i, own, :], acts, LAST)
            part = dot(message_v[rows:, span], acts).astype(BF16)
            for k in range(fan):
                send_v[i * fan + k, own, :] = part[:, k * take : (k + 1) * take]
        there = (pl.ds(i * fan, fan), pl.ds(0, ranks))
        outs.append(pltpu.make_async_copy(send_v.at[there], send_ref.at[there], out_sems.at[2 + i]))
        outs[-1].start()
    parts = []
    for b in range(blocks):
        span = slice(b * BLOCK_ROWS, (b + 1) * BLOCK_ROWS)
        low = low_v[b * RANK : (b + 1) * RANK, :].astype(BF16)
        parts.append(adapter_scale * dot(low, message_v[span, :]))
    part = jnp.concatenate(parts, axis=0)
    width = depth // groups
    lane = lax.broadcasted_iota(jnp.int32, (8, 128), 1) // width
    row = lax.broadcasted_iota(jnp.int32, (8, take), 0)
    turn = lax.broadcasted_iota(jnp.int32, (8, take), 1) // RANK % blocks
    slots = jnp.zeros((8, take), F32)
    for b in range(blocks):
        here = ((row == 0) & (turn == b)) | (row == 1 + b)
        slots = jnp.where(here, table_ref[ids_ref[0, b]].astype(F32), slots)
    fit = 128 // width
    for d in range(groups):
        column, mine = d // fit, d % fit
        halves = []
        for h in range(take // 128):
            total = jnp.zeros((8, 128), F32)
            for g in range(fit):
                k = h * fit + g
                tile = part[8 * k : 8 * k + 8, 128 * column : 128 * column + 128]
                tile = pltpu.roll(tile, ((g - mine) * width) % 128, 1)
                total = jnp.where(lane == g, tile, total)
            halves.append(total)
        packed = jnp.concatenate([jnp.concatenate(halves, axis=1), slots], axis=0)
        send_v[d, ranks:, :] = packed.astype(BF16)
    there = (pl.ds(0, groups), pl.ds(ranks, 16))
    outs.append(pltpu.make_async_copy(send_v.at[there], send_ref.at[there], out_sems.at[2 + chunks]))
    outs[-1].start()
    for out in outs:
        out.wait()


def front(count, ids, table, grad, up, acts, down, groups):
    blocks = count.shape[1]
    rows, width = acts.shape
    depth = grad.shape[1]
    wide = depth
    chunks = width // wide
    ranks = blocks * RANK
    shape = jax.ShapeDtypeStruct
    hbm = pl.BlockSpec(memory_space=HBM)
    send = shape((groups, ranks + 16, width // groups), BF16)
    return pl.pallas_call(
        front_kernel,
        out_shape=(
            shape((EARLY, depth), BF16),
            shape((rows + RANK - EARLY + chunks * ranks, depth), BF16),
            send,
        ),
        in_specs=[hbm] * 7,
        out_specs=(hbm,) * 3,
        scratch_shapes=[
            pltpu.SMEM(count.shape, jnp.int32),
            pltpu.SMEM(ids.shape, jnp.int32),
            pltpu.SMEM(table.shape, jnp.int32),
            pltpu.VMEM((rows, depth), BF16),
            pltpu.VMEM((ranks, depth), BF16),
            pltpu.VMEM((chunks, rows, wide), BF16),
            pltpu.VMEM((chunks, ranks, wide), BF16),
            pltpu.VMEM((ranks, BLOCK_ROWS), F32),
            pltpu.VMEM((rows + RANK, depth), BF16),
            pltpu.VMEM(send.shape, BF16),
            pltpu.SemaphoreType.DMA((5,)),
            pltpu.SemaphoreType.DMA((chunks,)),
            pltpu.SemaphoreType.DMA((chunks,)),
            pltpu.SemaphoreType.DMA((chunks + 3,)),
            pltpu.SemaphoreType.DMA((chunks,)),
        ],
        compiler_params=vmem(18),
        cost_estimate=pl.CostEstimate(flops=10**10, transcendentals=0, bytes_accessed=3 * rows * width),
        name="front",
    )(*in_hbm(count, ids, table, grad, up, acts, down))


def join_kernel(counts, spots_ref, *refs):
    parts, outs = refs[: sum(counts)], refs[sum(counts) :]
    i = 0
    for n, out in zip(counts, outs):
        rows = parts[i].shape[0]
        for part in parts[i : i + n]:
            at = pl.multiple_of(spots_ref[i] * rows, rows)
            out[pl.ds(at, rows), :] = part[...]
            i += 1


def join(spots, *groups):
    counts = tuple(len(g) for g in groups)
    in_vmem = pl.BlockSpec(memory_space=pltpu.VMEM)
    return pl.pallas_call(
        functools.partial(join_kernel, counts),
        out_shape=[jax.ShapeDtypeStruct((sum(v.shape[0] for v in g), g[0].shape[1]), BF16) for g in groups],
        in_specs=[pl.BlockSpec(memory_space=pltpu.SMEM)] + [in_vmem] * sum(counts),
        out_specs=[in_vmem] * len(groups),
        compiler_params=vmem(4),
        cost_estimate=pl.CostEstimate(flops=10**6, transcendentals=0, bytes_accessed=1 << 21),
        name="join",
    )(spots, *[v for g in groups for v in g])


def collect_kernel(got_h, out_a, out_b, a_v, tail_v, pick_v, sems):
    sources, ranks, take = a_v.shape
    adapters = out_a.shape[0]
    blocks = ranks // RANK
    ins = [
        pltpu.make_async_copy(got_h.at[pl.ds(0, sources), pl.ds(ranks, 16)], tail_v, sems.at[0]),
        pltpu.make_async_copy(got_h.at[pl.ds(0, sources), pl.ds(0, ranks)], a_v, sems.at[1]),
    ]
    for copy in ins:
        copy.start()
    ins[0].wait()
    tail = tail_v[...].astype(F32)
    lane = lax.broadcasted_iota(jnp.int32, (RANK, 128), 1)
    same = lane % RANK == lax.broadcasted_iota(jnp.int32, (RANK, 128), 0)
    fit = 128 // ranks
    for v in range(sources // fit):
        slots = jnp.broadcast_to(tail[v * fit, 8:9, :128], (RANK, 128))
        for k in range(1, fit):
            row = jnp.broadcast_to(tail[v * fit + k, 8:9, :128], (RANK, 128))
            slots = jnp.where(lane // ranks == k, row, slots)
        slots = jnp.where(same, slots, -1.0)
        for j in range(adapters):
            pick = jnp.where(slots == float(j), 1.0, 0.0).astype(BF16)
            pick_v[j * RANK : (j + 1) * RANK, v * 128 : (v + 1) * 128] = pick
    ins[1].wait()
    total = dot(pick_v[...], a_v[...].reshape(sources * ranks, take))
    out_a[...] = total.reshape(adapters, RANK, take).astype(BF16)

    width = out_b.shape[1]
    terms = tail[:, :8, :].reshape(sources * 8, take).astype(BF16)
    lane = lax.broadcasted_iota(jnp.int32, (adapters, sources * 8), 1)
    slot = lax.broadcasted_iota(jnp.int32, (adapters, sources * 8), 0).astype(F32)
    sums = []
    for b in range(blocks):
        slots = jnp.zeros((1, sources * 8), F32)
        for source in range(sources):
            slots = jnp.where(lane[:1] // 8 == source, tail[source, 9 + b : 10 + b, : sources * 8], slots)
        hit = slots == slot
        pick = jnp.concatenate([jnp.where(hit & (lane % 8 == r), 1.0, 0.0) for r in range(8)], axis=0)
        at = b * 2 * width
        total = dot(pick.astype(BF16), terms[:, at // 128 * 128 : at // 128 * 128 + 128])
        sums.append(pltpu.roll(total, (128 - at % 128) % 128, 1))
    total = sums[0]
    for more in sums[1:]:
        total = total + more
    for r in range(8):
        turned = total[r * adapters : (r + 1) * adapters, :].T
        out_b[r] = turned[:width].astype(BF16)
        out_b[8 + r] = turned[width : 2 * width].astype(BF16)


def collect(got, adapters, blocks, depth):
    groups, _, take = got.shape
    ranks = blocks * RANK
    in_vmem = pl.BlockSpec(memory_space=pltpu.VMEM)
    return pl.pallas_call(
        collect_kernel,
        out_shape=(
            jax.ShapeDtypeStruct((adapters, RANK, take), BF16),
            jax.ShapeDtypeStruct((RANK, depth // groups, adapters), BF16),
        ),
        in_specs=[pl.BlockSpec(memory_space=HBM)],
        out_specs=(in_vmem, in_vmem),
        scratch_shapes=[
            pltpu.VMEM((groups, ranks, take), BF16),
            pltpu.VMEM((groups, 16, take), BF16),
            pltpu.VMEM((adapters * RANK, groups * ranks), BF16),
            pltpu.SemaphoreType.DMA((2,)),
        ],
        compiler_params=vmem(20),
        cost_estimate=pl.CostEstimate(flops=4 * 10**9, transcendentals=0, bytes_accessed=4 * got.size),
        name="collect",
    )(*in_hbm(got))


def unpack_kernel(early_ref, late_ref, message_ref, low_ref, down_ref):
    rows = message_ref.shape[0]
    ranks = low_ref.shape[1]
    rest = rows - EARLY
    message_ref[:EARLY, :] = early_ref[...]
    message_ref[EARLY:, :] = late_ref[:rest, :]
    down_ref[...] = late_ref[rest + RANK :, :]
    low = jnp.concatenate([late_ref[rest : rest + RANK, :rows].astype(F32)] * (ranks // RANK), axis=0)
    own = lax.broadcasted_iota(jnp.int32, low.shape, 0) // RANK
    of = lax.broadcasted_iota(jnp.int32, low.shape, 1) // BLOCK_ROWS
    low_ref[...] = jnp.where(own == of, low, 0.0).T.astype(BF16)


def unpack(early, late, rows, ranks):
    depth = early.shape[1]
    shape = jax.ShapeDtypeStruct
    in_vmem = pl.BlockSpec(memory_space=pltpu.VMEM)
    return pl.pallas_call(
        unpack_kernel,
        out_shape=(
            shape((rows, depth), BF16),
            shape((rows, ranks), BF16),
            shape((late.shape[0] + EARLY - rows - RANK, depth), BF16),
        ),
        in_specs=[in_vmem] * 2,
        out_specs=(in_vmem,) * 3,
        compiler_params=vmem(4),
        name="unpack",
    )(early, late)


def product_kernel(which, alias, starts_ref, message_ref, low_ref, down_ref, *refs):
    n = len(which)
    blocks = refs[:n]
    out_ref, out_v, out_sems = refs[n + alias :]
    ranks, wide = low_ref.shape[1], down_ref.shape[1]
    outs = []
    for i in range(n):
        start = pl.multiple_of(starts_ref[which[i]], BLOCK)
        chunk = pl.ds(pl.multiple_of(start // wide * ranks, ranks), ranks)
        down = down_ref[chunk, pl.ds(pl.multiple_of(start % wide, BLOCK), BLOCK)]
        total = dot(message_ref[...], blocks[i][...], LAST) + dot(low_ref[...], down)
        out_v[i] = total.astype(BF16)
        out = pltpu.make_async_copy(out_v.at[i], out_ref.at[:, pl.ds(start, BLOCK)], out_sems.at[i])
        out.start()
        outs.append(out)
    for out in outs:
        out.wait()


def product(blocks, starts, message, low, down, before, name):
    n = len(blocks)
    rows, depth = message.shape
    width = down.size // low.shape[1]
    operands = [starts, message, low, down, *[b[0] for b in blocks]]
    in_vmem = pl.BlockSpec(memory_space=pltpu.VMEM)
    in_specs = [pl.BlockSpec(memory_space=pltpu.SMEM)] + [in_vmem] * (len(operands) - 1)
    hbm = pl.BlockSpec(memory_space=HBM)
    if before is not None:
        operands += in_hbm(before)
        in_specs.append(hbm)
    columns = n * BLOCK
    return pl.pallas_call(
        functools.partial(product_kernel, tuple(b[1] for b in blocks), before is not None),
        out_shape=jax.ShapeDtypeStruct((rows, width), BF16),
        in_specs=in_specs,
        out_specs=hbm,
        scratch_shapes=[pltpu.VMEM((n, rows, BLOCK), BF16), pltpu.SemaphoreType.DMA((n,))],
        input_output_aliases={} if before is None else {len(operands) - 1: 0},
        compiler_params=vmem(12),
        cost_estimate=pl.CostEstimate(
            flops=10**6, transcendentals=0, bytes_accessed=10**6
        ),
        name=name,
    )(*operands)


def spot(at, core):
    return (at + core) % SIDE


def near(at, core):
    return ((spot(at, core) ^ 1) - core) % SIDE


def far(at, core):
    return (SIDE - 1 - spot(at, core) - core) % SIDE


def moved(array, to):
    route = []
    for d in range(SIDE * SIDE * CORES):
        x, z, core = to(d // (SIDE * CORES), d // CORES % SIDE, d % CORES)
        route.append((d, (x * SIDE + z) * CORES + core))
    return lax.ppermute(array, "dp", route)


def x_near(x, z, core):
    return near(x, core), z, core


def x_far(x, z, core):
    return far(x, core), z, core


def z_near(x, z, core):
    return x, near(z, core), core


def z_far(x, z, core):
    return x, far(z, core), core


def other_core(x, z, core):
    return x, z, 1 - core


def places(line, core):
    steps = (line, near(line, core), far(line, core), near(far(line, core), core))
    return [(s * CORES + core) * BLOCK for s in steps]


def hop(x, route):
    return lax.ppermute(x, "pipe", route)


def tie(*arrays):
    return lax.optimization_barrier(arrays)


def body(
    acts,
    output_gradient,
    frozen_value_weight,
    adapter_down_weight,
    adapter_up_weight,
    block_adapter_index,
    token_row_count,
    adapter_slot_table,
):
    blocks = token_row_count.shape[1]
    rows, width = acts.shape[1:]
    depth = output_gradient.shape[2]
    adapters = adapter_slot_table.shape[0]
    groups = lax.axis_size("dp")
    down = adapter_down_weight.reshape(blocks * RANK, width)
    up = adapter_up_weight.reshape(blocks * RANK, depth)
    half = width // 2
    me = lax.axis_index("dp")
    x, z, core = me // (SIDE * CORES), me // CORES % SIDE, me % CORES
    back = [(1, 0), (2, 1), (3, 2)]

    piece_a = lax.dynamic_slice_in_dim(
        frozen_value_weight[0], ((z * CORES + core) * SIDE + spot(x, core)) * PIECE, PIECE, 0
    )
    piece_b = lax.dynamic_slice_in_dim(
        frozen_value_weight[0], half + ((x * CORES + core) * SIDE + spot(z, core)) * PIECE, PIECE, 0
    )
    a0, b0 = hop(piece_a, back), hop(piece_b, back)
    early, late, send = front(
        token_row_count, block_adapter_index, adapter_slot_table,
        output_gradient[0], up, acts[0], down, groups,
    )
    spot_a, spot_b = spot(x, core), spot(z, core)
    halves = jnp.stack([spot_a % 2, 1 - spot_a % 2, spot_b % 2, 1 - spot_b % 2]).astype(jnp.int32)
    wholes = jnp.stack([spot_a // 2, 1 - spot_a // 2, spot_b // 2, 1 - spot_b // 2]).astype(jnp.int32)
    starts = []
    for c in (core, 1 - core):
        starts += places(z, c) + [half + s for s in places(x, c)]
    starts = jnp.stack(starts).astype(jnp.int32)
    a0, b0, send, early, late, halves, wholes, starts = tie(
        a0, b0, send, early, late, halves, wholes, starts
    )

    a1, b1 = moved(a0, x_near), moved(b0, z_near)
    early = hop(early, back)
    a0, b0, a1, b1, send, late = tie(a0, b0, a1, b1, send, late)

    got = lax.all_to_all(send, "dp", split_axis=0, concat_axis=0, tiled=True)
    ap, bp = join(halves, (a0, a1), (b0, b1))
    aq, bq = moved(ap, x_far), moved(bp, z_far)
    aq, bq, early, late = tie(aq, bq, early, late)

    late = hop(late, back)
    a, b = join(wholes, (ap, aq), (bp, bq))
    a_near, b_near = moved(a, z_near), moved(b, x_near)
    a_far, b_far = moved(a, z_far), moved(b, x_far)
    total_a, total_b = collect(got, adapters, blocks, depth)
    a, b, a_near, b_near, a_far, b_far, total_a, total_b = tie(
        a, b, a_near, b_near, a_far, b_far, total_a, total_b
    )

    def pair(a, b, step, mine=True):
        at = step if mine else step + 2 * SIDE
        return [(a, at), (b, at + SIDE)]

    def others(a, b, step):
        return pair(moved(a, other_core), moved(b, other_core), step, False)

    a_last, b_last = moved(a_near, z_far), moved(b_near, x_far)
    message, low, down = unpack(early, late, rows, blocks * RANK)
    message, a, b, a_near = tie(message, a, b, a_near)
    shared = (starts, message, low, down)
    mine = pair(a, b, 0) + pair(a_near, b_near, 1) + pair(a_far, b_far, 2)
    received = product(mine, *shared, None, "product_mine")
    a_other, b_other, a_near_other = [moved(v, other_core) for v in (a, b, a_near)]
    received, a_other, b_other, a_near_other, b_near, a_far, b_far = tie(
        received, a_other, b_other, a_near_other, b_near, a_far, b_far
    )
    first = pair(a_other, b_other, 0, False) + [(a_near_other, 1 + 2 * SIDE)]
    second = [(moved(b_near, other_core), 1 + 3 * SIDE)] + others(a_far, b_far, 2)
    received = product(first, *shared, received, "product_first")
    received, a_last, b_last = tie(received, a_last, b_last)
    theirs = others(a_last, b_last, 3)
    received = product(second + pair(a_last, b_last, 3), *shared, received, "product_second")
    received = product(theirs, *shared, received, "product_end")
    return received[None], total_a[None], jnp.transpose(total_b, (2, 0, 1))[None]


def solution(mesh):
    in_specs = (
        P("pipe", "dp", None),
        P("pipe", "dp", None),
        P("pipe", None, None),
        P("pipe", "dp", None, None),
        P("pipe", "dp", None, None),
        P("pipe", "dp"),
        P("pipe", "dp"),
        P(),
    )
    out_specs = (P("pipe", "dp", None), P("pipe", None, None, "dp"), P("pipe", None, None, "dp"))
    return jax.shard_map(body, mesh=mesh, in_specs=in_specs, out_specs=out_specs, check_vma=False)
```

```python
import functools

import jax
import jax.numpy as jnp
from jax import lax
from jax.experimental import pallas as pl
from jax.experimental.pallas import tpu as pltpu
from jax.sharding import PartitionSpec as P

BLOCK_ROWS = 128
RANK = 16
BF16 = jnp.bfloat16
F32 = jnp.float32

adapter_scale = 2.0

SIDE, CORES = 4, 2
PIECE = 128
BLOCK = SIDE * PIECE
EARLY = 320
HBM = pltpu.MemorySpace.HBM

LAST = (((1,), (1,)), ((), ()))
FIRST = (((0,), (0,)), ((), ()))


def dot(a, b, dims=(((1,), (0,)), ((), ()))):
    return lax.dot_general(a, b, dims, preferred_element_type=F32)


def vmem(mib):
    return pltpu.CompilerParams(vmem_limit_bytes=mib << 20)


def in_hbm(*arrays):
    return [pltpu.with_memory_space_constraint(a, HBM) for a in arrays]


def front_kernel(count_h, ids_h, table_h, grad_ref, up_ref, acts_ref, down_ref, early_ref, late_ref,
                 send_ref, count_ref, ids_ref, table_ref, grad_v, up_v, acts_v, down_v, low_v,
                 message_v, send_v, in_sems, acts_sems, down_sems, out_sems, down_out_sems):
    blocks = count_ref.shape[1]
    rows, depth = grad_v.shape
    chunks, _, wide = acts_v.shape
    groups, _, take = send_v.shape
    ranks = blocks * RANK
    ins = [
        pltpu.make_async_copy(count_h, count_ref, in_sems.at[0]),
        pltpu.make_async_copy(grad_ref, grad_v, in_sems.at[1]),
        pltpu.make_async_copy(up_ref, up_v, in_sems.at[2]),
        pltpu.make_async_copy(ids_h, ids_ref, in_sems.at[3]),
        pltpu.make_async_copy(table_h, table_ref, in_sems.at[4]),
    ]
    for copy in ins:
        copy.start()
    acts_in, down_in = [], []
    for i in range(chunks):
        span = pl.ds(i * wide, wide)
        acts_in.append(pltpu.make_async_copy(acts_ref.at[:, span], acts_v.at[i], acts_sems.at[i]))
        down_in.append(pltpu.make_async_copy(down_ref.at[:, span], down_v.at[i], down_sems.at[i]))
        down_in[i].start()
        acts_in[i].start()
    message_v[rows:, :] = jnp.zeros((RANK, depth), BF16)
    for copy in ins:
        copy.wait()
    for b in range(blocks):
        span = slice(b * BLOCK_ROWS, (b + 1) * BLOCK_ROWS)
        at = lax.broadcasted_iota(jnp.int32, (BLOCK_ROWS, depth), 0)
        masked = jnp.where(at < count_ref[0, b], grad_v[span, :].astype(F32), 0.0).astype(BF16)
        message_v[span, :] = masked
        low = dot(up_v[b * RANK : (b + 1) * RANK, :], masked, LAST)
        message_v[rows:, span] = (adapter_scale * low).astype(BF16)
    rest = rows + RANK - EARLY
    outs = [
        pltpu.make_async_copy(message_v.at[pl.ds(0, EARLY)], early_ref, out_sems.at[0]),
        pltpu.make_async_copy(message_v.at[pl.ds(EARLY, rest)], late_ref.at[pl.ds(0, rest)], out_sems.at[1]),
    ]
    for out in outs:
        out.start()
    low_v[...] = jnp.zeros_like(low_v)
    fan = wide // take
    for i in range(chunks):
        acts_in[i].wait()
        down_in[i].wait()
        outs.append(pltpu.make_async_copy(
            down_v.at[i], late_ref.at[pl.ds(rest + i * ranks, ranks)], down_out_sems.at[i]
        ))
        outs[-1].start()
        for b in range(blocks):
            span = slice(b * BLOCK_ROWS, (b + 1) * BLOCK_ROWS)
            own = slice(b * RANK, (b + 1) * RANK)
            acts = acts_v[i, span, :]
            low_v[own, :] += dot(down_v[i, own, :], acts, LAST)
            part = dot(message_v[rows:, span], acts).astype(BF16)
            for k in range(fan):
                send_v[i * fan + k, own, :] = part[:, k * take : (k + 1) * take]
        there = (pl.ds(i * fan, fan), pl.ds(0, ranks))
        outs.append(pltpu.make_async_copy(send_v.at[there], send_ref.at[there], out_sems.at[2 + i]))
        outs[-1].start()
    parts = []
    for b in range(blocks):
        span = slice(b * BLOCK_ROWS, (b + 1) * BLOCK_ROWS)
        low = low_v[b * RANK : (b + 1) * RANK, :].astype(BF16)
        parts.append(adapter_scale * dot(low, message_v[span, :]))
    part = jnp.concatenate(parts, axis=0)
    width = depth // groups
    lane = lax.broadcasted_iota(jnp.int32, (8, 128), 1) // width
    row = lax.broadcasted_iota(jnp.int32, (8, take), 0)
    turn = lax.broadcasted_iota(jnp.int32, (8, take), 1) // RANK % blocks
    slots = jnp.zeros((8, take), F32)
    for b in range(blocks):
        here = ((row == 0) & (turn == b)) | (row == 1 + b)
        slots = jnp.where(here, table_ref[ids_ref[0, b]].astype(F32), slots)
    fit = 128 // width
    for d in range(groups):
        column, mine = d // fit, d % fit
        halves = []
        for h in range(take // 128):
            total = jnp.zeros((8, 128), F32)
            for g in range(fit):
                k = h * fit + g
                tile = part[8 * k : 8 * k + 8, 128 * column : 128 * column + 128]
                tile = pltpu.roll(tile, ((g - mine) * width) % 128, 1)
                total = jnp.where(lane == g, tile, total)
            halves.append(total)
        packed = jnp.concatenate([jnp.concatenate(halves, axis=1), slots], axis=0)
        send_v[d, ranks:, :] = packed.astype(BF16)
    there = (pl.ds(0, groups), pl.ds(ranks, 16))
    outs.append(pltpu.make_async_copy(send_v.at[there], send_ref.at[there], out_sems.at[2 + chunks]))
    outs[-1].start()
    for out in outs:
        out.wait()


def front(count, ids, table, grad, up, acts, down, groups):
    blocks = count.shape[1]
    rows, width = acts.shape
    depth = grad.shape[1]
    wide = depth
    chunks = width // wide
    ranks = blocks * RANK
    shape = jax.ShapeDtypeStruct
    hbm = pl.BlockSpec(memory_space=HBM)
    send = shape((groups, ranks + 16, width // groups), BF16)
    return pl.pallas_call(
        front_kernel,
        out_shape=(
            HBM((EARLY, depth), BF16),
            HBM((rows + RANK - EARLY + chunks * ranks, depth), BF16),
            HBM(send.shape, BF16),
        ),
        in_specs=[hbm] * 7,
        out_specs=(hbm,) * 3,
        scratch_shapes=[
            pltpu.SMEM(count.shape, jnp.int32),
            pltpu.SMEM(ids.shape, jnp.int32),
            pltpu.SMEM(table.shape, jnp.int32),
            pltpu.VMEM((rows, depth), BF16),
            pltpu.VMEM((ranks, depth), BF16),
            pltpu.VMEM((chunks, rows, wide), BF16),
            pltpu.VMEM((chunks, ranks, wide), BF16),
            pltpu.VMEM((ranks, BLOCK_ROWS), F32),
            pltpu.VMEM((rows + RANK, depth), BF16),
            pltpu.VMEM(send.shape, BF16),
            pltpu.SemaphoreType.DMA((5,)),
            pltpu.SemaphoreType.DMA((chunks,)),
            pltpu.SemaphoreType.DMA((chunks,)),
            pltpu.SemaphoreType.DMA((chunks + 3,)),
            pltpu.SemaphoreType.DMA((chunks,)),
        ],
        compiler_params=vmem(18),
        cost_estimate=pl.CostEstimate(flops=10**10, transcendentals=0, bytes_accessed=3 * rows * width),
        name="front",
    )(*in_hbm(count, ids, table, grad, up, acts, down))


def join_kernel(counts, spots_ref, *refs):
    parts, outs = refs[: sum(counts)], refs[sum(counts) :]
    i = 0
    for n, out in zip(counts, outs):
        rows = parts[i].shape[0]
        for part in parts[i : i + n]:
            at = pl.multiple_of(spots_ref[i] * rows, rows)
            out[pl.ds(at, rows), :] = part[...]
            i += 1


def join(spots, *groups):
    counts = tuple(len(g) for g in groups)
    in_vmem = pl.BlockSpec(memory_space=pltpu.VMEM)
    return pl.pallas_call(
        functools.partial(join_kernel, counts),
        out_shape=[jax.ShapeDtypeStruct((sum(v.shape[0] for v in g), g[0].shape[1]), BF16) for g in groups],
        in_specs=[pl.BlockSpec(memory_space=pltpu.SMEM)] + [in_vmem] * sum(counts),
        out_specs=[in_vmem] * len(groups),
        compiler_params=vmem(4),
        cost_estimate=pl.CostEstimate(flops=10**6, transcendentals=0, bytes_accessed=1 << 21),
        name="join",
    )(spots, *[v for g in groups for v in g])


def collect_kernel(got_h, out_a, out_b, a_v, tail_v, pick_v, sems):
    sources, ranks, take = a_v.shape
    adapters = out_a.shape[0]
    blocks = ranks // RANK
    ins = [
        pltpu.make_async_copy(got_h.at[pl.ds(0, sources), pl.ds(ranks, 16)], tail_v, sems.at[0]),
        pltpu.make_async_copy(got_h.at[pl.ds(0, sources), pl.ds(0, ranks)], a_v, sems.at[1]),
    ]
    for copy in ins:
        copy.start()
    ins[0].wait()
    tail = tail_v[...].astype(F32)
    lane = lax.broadcasted_iota(jnp.int32, (RANK, 128), 1)
    same = lane % RANK == lax.broadcasted_iota(jnp.int32, (RANK, 128), 0)
    fit = 128 // ranks
    for v in range(sources // fit):
        slots = jnp.broadcast_to(tail[v * fit, 8:9, :128], (RANK, 128))
        for k in range(1, fit):
            row = jnp.broadcast_to(tail[v * fit + k, 8:9, :128], (RANK, 128))
            slots = jnp.where(lane // ranks == k, row, slots)
        slots = jnp.where(same, slots, -1.0)
        for j in range(adapters):
            pick = jnp.where(slots == float(j), 1.0, 0.0).astype(BF16)
            pick_v[j * RANK : (j + 1) * RANK, v * 128 : (v + 1) * 128] = pick
    ins[1].wait()
    total = dot(pick_v[...], a_v[...].reshape(sources * ranks, take))
    out_a[...] = total.reshape(adapters, RANK, take).astype(BF16)

    width = out_b.shape[1]
    terms = tail[:, :8, :].reshape(sources * 8, take).astype(BF16)
    lane = lax.broadcasted_iota(jnp.int32, (adapters, sources * 8), 1)
    slot = lax.broadcasted_iota(jnp.int32, (adapters, sources * 8), 0).astype(F32)
    sums = []
    for b in range(blocks):
        slots = jnp.zeros((1, sources * 8), F32)
        for source in range(sources):
            slots = jnp.where(lane[:1] // 8 == source, tail[source, 9 + b : 10 + b, : sources * 8], slots)
        hit = slots == slot
        pick = jnp.concatenate([jnp.where(hit & (lane % 8 == r), 1.0, 0.0) for r in range(8)], axis=0)
        at = b * 2 * width
        total = dot(pick.astype(BF16), terms[:, at // 128 * 128 : at // 128 * 128 + 128])
        sums.append(pltpu.roll(total, (128 - at % 128) % 128, 1))
    total = sums[0]
    for more in sums[1:]:
        total = total + more
    for r in range(8):
        turned = total[r * adapters : (r + 1) * adapters, :].T
        out_b[r] = turned[:width].astype(BF16)
        out_b[8 + r] = turned[width : 2 * width].astype(BF16)


def collect(got, adapters, blocks, depth):
    groups, _, take = got.shape
    ranks = blocks * RANK
    in_vmem = pl.BlockSpec(memory_space=pltpu.VMEM)
    return pl.pallas_call(
        collect_kernel,
        out_shape=(
            jax.ShapeDtypeStruct((adapters, RANK, take), BF16),
            jax.ShapeDtypeStruct((RANK, depth // groups, adapters), BF16),
        ),
        in_specs=[pl.BlockSpec(memory_space=HBM)],
        out_specs=(in_vmem, in_vmem),
        scratch_shapes=[
            pltpu.VMEM((groups, ranks, take), BF16),
            pltpu.VMEM((groups, 16, take), BF16),
            pltpu.VMEM((adapters * RANK, groups * ranks), BF16),
            pltpu.SemaphoreType.DMA((2,)),
        ],
        compiler_params=vmem(20),
        cost_estimate=pl.CostEstimate(flops=4 * 10**9, transcendentals=0, bytes_accessed=4 * got.size),
        name="collect",
    )(*in_hbm(got))


def unpack_kernel(early_ref, late_ref, message_ref, low_ref, down_ref):
    rows = message_ref.shape[0]
    ranks = low_ref.shape[1]
    rest = rows - EARLY
    message_ref[:EARLY, :] = early_ref[...]
    message_ref[EARLY:, :] = late_ref[:rest, :]
    down_ref[...] = late_ref[rest + RANK :, :]
    low = jnp.concatenate([late_ref[rest : rest + RANK, :rows].astype(F32)] * (ranks // RANK), axis=0)
    own = lax.broadcasted_iota(jnp.int32, low.shape, 0) // RANK
    of = lax.broadcasted_iota(jnp.int32, low.shape, 1) // BLOCK_ROWS
    low_ref[...] = jnp.where(own == of, low, 0.0).T.astype(BF16)


def unpack(early, late, rows, ranks):
    depth = early.shape[1]
    shape = jax.ShapeDtypeStruct
    in_vmem = pl.BlockSpec(memory_space=pltpu.VMEM)
    return pl.pallas_call(
        unpack_kernel,
        out_shape=(
            shape((rows, depth), BF16),
            shape((rows, ranks), BF16),
            shape((late.shape[0] + EARLY - rows - RANK, depth), BF16),
        ),
        in_specs=[in_vmem] * 2,
        out_specs=(in_vmem,) * 3,
        compiler_params=vmem(4),
        name="unpack",
    )(early, late)


def product_kernel(which, alias, starts_ref, message_ref, low_ref, down_ref, *refs):
    n = len(which)
    blocks = refs[:n]
    out_ref, out_v, out_sems = refs[n + alias :]
    ranks, wide = low_ref.shape[1], down_ref.shape[1]
    outs = []
    for i in range(n):
        start = pl.multiple_of(starts_ref[which[i]], BLOCK)
        chunk = pl.ds(pl.multiple_of(start // wide * ranks, ranks), ranks)
        down = down_ref[chunk, pl.ds(pl.multiple_of(start % wide, BLOCK), BLOCK)]
        total = dot(message_ref[...], blocks[i][...], LAST) + dot(low_ref[...], down)
        out_v[i] = total.astype(BF16)
        out = pltpu.make_async_copy(out_v.at[i], out_ref.at[:, pl.ds(start, BLOCK)], out_sems.at[i])
        out.start()
        outs.append(out)
    for out in outs:
        out.wait()


def product(blocks, starts, message, low, down, before, name):
    n = len(blocks)
    rows, depth = message.shape
    width = down.size // low.shape[1]
    operands = [starts, message, low, down, *[b[0] for b in blocks]]
    in_vmem = pl.BlockSpec(memory_space=pltpu.VMEM)
    in_specs = [pl.BlockSpec(memory_space=pltpu.SMEM)] + [in_vmem] * (len(operands) - 1)
    hbm = pl.BlockSpec(memory_space=HBM)
    if before is not None:
        operands += in_hbm(before)
        in_specs.append(hbm)
    columns = n * BLOCK
    return pl.pallas_call(
        functools.partial(product_kernel, tuple(b[1] for b in blocks), before is not None),
        out_shape=jax.ShapeDtypeStruct((rows, width), BF16),
        in_specs=in_specs,
        out_specs=hbm,
        scratch_shapes=[pltpu.VMEM((n, rows, BLOCK), BF16), pltpu.SemaphoreType.DMA((n,))],
        input_output_aliases={} if before is None else {len(operands) - 1: 0},
        compiler_params=vmem(12),
        cost_estimate=pl.CostEstimate(
            flops=10**6, transcendentals=0, bytes_accessed=10**6
        ),
        name=name,
    )(*operands)


def spot(at, core):
    return (at + core) % SIDE


def near(at, core):
    return ((spot(at, core) ^ 1) - core) % SIDE


def far(at, core):
    return (SIDE - 1 - spot(at, core) - core) % SIDE


def moved(array, to):
    route = []
    for d in range(SIDE * SIDE * CORES):
        x, z, core = to(d // (SIDE * CORES), d // CORES % SIDE, d % CORES)
        route.append((d, (x * SIDE + z) * CORES + core))
    return lax.ppermute(array, "dp", route)


def x_near(x, z, core):
    return near(x, core), z, core


def x_far(x, z, core):
    return far(x, core), z, core


def z_near(x, z, core):
    return x, near(z, core), core


def z_far(x, z, core):
    return x, far(z, core), core


def other_core(x, z, core):
    return x, z, 1 - core


def places(line, core):
    steps = (line, near(line, core), far(line, core), near(far(line, core), core))
    return [(s * CORES + core) * BLOCK for s in steps]


def hop(x, route):
    return lax.ppermute(x, "pipe", route)


def tie(*arrays):
    return lax.optimization_barrier(arrays)


def body(
    acts,
    output_gradient,
    frozen_value_weight,
    adapter_down_weight,
    adapter_up_weight,
    block_adapter_index,
    token_row_count,
    adapter_slot_table,
):
    blocks = token_row_count.shape[1]
    rows, width = acts.shape[1:]
    depth = output_gradient.shape[2]
    adapters = adapter_slot_table.shape[0]
    groups = lax.axis_size("dp")
    down = adapter_down_weight.reshape(blocks * RANK, width)
    up = adapter_up_weight.reshape(blocks * RANK, depth)
    half = width // 2
    me = lax.axis_index("dp")
    x, z, core = me // (SIDE * CORES), me // CORES % SIDE, me % CORES
    back = [(1, 0), (2, 1), (3, 2)]

    piece_a = lax.dynamic_slice_in_dim(
        frozen_value_weight[0], ((z * CORES + core) * SIDE + spot(x, core)) * PIECE, PIECE, 0
    )
    piece_b = lax.dynamic_slice_in_dim(
        frozen_value_weight[0], half + ((x * CORES + core) * SIDE + spot(z, core)) * PIECE, PIECE, 0
    )
    a0, b0 = hop(piece_a, back), hop(piece_b, back)
    early, late, send = front(
        token_row_count, block_adapter_index, adapter_slot_table,
        output_gradient[0], up, acts[0], down, groups,
    )
    spot_a, spot_b = spot(x, core), spot(z, core)
    halves_a = jnp.stack([spot_a % 2, 1 - spot_a % 2]).astype(jnp.int32)
    halves_b = jnp.stack([spot_b % 2, 1 - spot_b % 2]).astype(jnp.int32)
    wholes = jnp.stack([spot_a // 2, 1 - spot_a // 2, spot_b // 2, 1 - spot_b // 2]).astype(jnp.int32)
    starts = []
    for c in (core, 1 - core):
        starts += places(z, c) + [half + s for s in places(x, c)]
    starts = jnp.stack(starts).astype(jnp.int32)
    a0, b0, send, early, late, halves_a, halves_b, wholes, starts = tie(
        a0, b0, send, early, late, halves_a, halves_b, wholes, starts
    )

    a1, b1 = moved(a0, x_near), moved(b0, z_near)
    early = hop(early, back)
    b0, b1, send, late = tie(b0, b1, send, late)

    got = lax.all_to_all(send, "dp", split_axis=0, concat_axis=0, tiled=True)
    ap, = join(halves_a, (a0, a1))
    bp, = join(halves_b, (b0, b1))
    aq, bq = moved(ap, x_far), moved(bp, z_far)
    aq, bq, early, late = tie(aq, bq, early, late)

    late = hop(late, back)
    a, b = join(wholes, (ap, aq), (bp, bq))
    a_near, b_near = moved(a, z_near), moved(b, x_near)
    a_far, b_far = moved(a, z_far), moved(b, x_far)
    total_a, total_b = collect(got, adapters, blocks, depth)
    a, b, a_near, b_near, total_a, total_b = tie(a, b, a_near, b_near, total_a, total_b)

    def pair(a, b, step, mine=True):
        at = step if mine else step + 2 * SIDE
        return [(a, at), (b, at + SIDE)]

    def others(a, b, step):
        return pair(moved(a, other_core), moved(b, other_core), step, False)

    a_last, b_last = moved(a_near, z_far), moved(b_near, x_far)
    late, a_far, b_far = tie(late, a_far, b_far)
    message, low, down = unpack(early, late, rows, blocks * RANK)
    message, a, b, a_near = tie(message, a, b, a_near)
    shared = (starts, message, low, down)
    mine = pair(a, b, 0) + pair(a_near, b_near, 1) + pair(a_far, b_far, 2)
    received = product(mine, *shared, None, "product_mine")
    a_other, b_other, a_near_other = [moved(v, other_core) for v in (a, b, a_near)]
    received, a_other, b_other, a_near_other, b_near, a_far, b_far = tie(
        received, a_other, b_other, a_near_other, b_near, a_far, b_far
    )
    first = pair(a_other, b_other, 0, False) + [(a_near_other, 1 + 2 * SIDE)]
    second = [(moved(b_near, other_core), 1 + 3 * SIDE)] + others(a_far, b_far, 2)
    received = product(first, *shared, received, "product_first")
    received, a_last, b_last = tie(received, a_last, b_last)
    theirs = others(a_last, b_last, 3)
    received = product(second + pair(a_last, b_last, 3), *shared, received, "product_second")
    received = product(theirs, *shared, received, "product_end")
    return received[None], total_a[None], jnp.transpose(total_b, (2, 0, 1))[None]


def solution(mesh):
    in_specs = (
        P("pipe", "dp", None),
        P("pipe", "dp", None),
        P("pipe", None, None),
        P("pipe", "dp", None, None),
        P("pipe", "dp", None, None),
        P("pipe", "dp"),
        P("pipe", "dp"),
        P(),
    )
    out_specs = (P("pipe", "dp", None), P("pipe", None, None, "dp"), P("pipe", None, None, "dp"))
    return jax.shard_map(body, mesh=mesh, in_specs=in_specs, out_specs=out_specs, check_vma=False)
```

```python
import functools

import jax
import jax.numpy as jnp
from jax import lax
from jax.experimental import pallas as pl
from jax.experimental.pallas import tpu as pltpu
from jax.sharding import PartitionSpec as P

BLOCK_ROWS = 128
RANK = 16
BF16 = jnp.bfloat16
F32 = jnp.float32

adapter_scale = 2.0

SIDE, CORES = 4, 2
PIECE = 128
BLOCK = SIDE * PIECE
EARLY = 352
HBM = pltpu.MemorySpace.HBM

LAST = (((1,), (1,)), ((), ()))
FIRST = (((0,), (0,)), ((), ()))


def dot(a, b, dims=(((1,), (0,)), ((), ()))):
    return lax.dot_general(a, b, dims, preferred_element_type=F32)


def vmem(mib):
    return pltpu.CompilerParams(vmem_limit_bytes=mib << 20)


def in_hbm(*arrays):
    return [pltpu.with_memory_space_constraint(a, HBM) for a in arrays]


def front_kernel(count_h, ids_h, table_h, grad_ref, up_ref, acts_ref, down_ref, early_ref, late_ref,
                 send_ref, count_ref, ids_ref, table_ref, grad_v, up_v, acts_v, down_v, low_v,
                 message_v, send_v, in_sems, acts_sems, down_sems, out_sems, down_out_sems):
    blocks = count_ref.shape[1]
    rows, depth = grad_v.shape
    chunks, _, wide = acts_v.shape
    groups, _, take = send_v.shape
    ranks = blocks * RANK
    ins = [
        pltpu.make_async_copy(count_h, count_ref, in_sems.at[0]),
        pltpu.make_async_copy(grad_ref, grad_v, in_sems.at[1]),
        pltpu.make_async_copy(up_ref, up_v, in_sems.at[2]),
        pltpu.make_async_copy(ids_h, ids_ref, in_sems.at[3]),
        pltpu.make_async_copy(table_h, table_ref, in_sems.at[4]),
    ]
    for copy in ins:
        copy.start()
    acts_in, down_in = [], []
    for i in range(chunks):
        span = pl.ds(i * wide, wide)
        acts_in.append(pltpu.make_async_copy(acts_ref.at[:, span], acts_v.at[i], acts_sems.at[i]))
        down_in.append(pltpu.make_async_copy(down_ref.at[:, span], down_v.at[i], down_sems.at[i]))
        down_in[i].start()
        acts_in[i].start()
    message_v[rows:, :] = jnp.zeros((RANK, depth), BF16)
    for copy in ins:
        copy.wait()
    for b in range(blocks):
        span = slice(b * BLOCK_ROWS, (b + 1) * BLOCK_ROWS)
        at = lax.broadcasted_iota(jnp.int32, (BLOCK_ROWS, depth), 0)
        masked = jnp.where(at < count_ref[0, b], grad_v[span, :].astype(F32), 0.0).astype(BF16)
        message_v[span, :] = masked
        low = dot(up_v[b * RANK : (b + 1) * RANK, :], masked, LAST)
        message_v[rows:, span] = (adapter_scale * low).astype(BF16)
    rest = rows + RANK - EARLY
    outs = [
        pltpu.make_async_copy(message_v.at[pl.ds(0, EARLY)], early_ref, out_sems.at[0]),
        pltpu.make_async_copy(message_v.at[pl.ds(EARLY, rest)], late_ref.at[pl.ds(0, rest)], out_sems.at[1]),
    ]
    for out in outs:
        out.start()
    low_v[...] = jnp.zeros_like(low_v)
    fan = wide // take
    for i in range(chunks):
        acts_in[i].wait()
        down_in[i].wait()
        outs.append(pltpu.make_async_copy(
            down_v.at[i], late_ref.at[pl.ds(rest + i * ranks, ranks)], down_out_sems.at[i]
        ))
        outs[-1].start()
        for b in range(blocks):
            span = slice(b * BLOCK_ROWS, (b + 1) * BLOCK_ROWS)
            own = slice(b * RANK, (b + 1) * RANK)
            acts = acts_v[i, span, :]
            low_v[own, :] += dot(down_v[i, own, :], acts, LAST)
            part = dot(message_v[rows:, span], acts).astype(BF16)
            for k in range(fan):
                send_v[i * fan + k, own, :] = part[:, k * take : (k + 1) * take]
        there = (pl.ds(i * fan, fan), pl.ds(0, ranks))
        outs.append(pltpu.make_async_copy(send_v.at[there], send_ref.at[there], out_sems.at[2 + i]))
        outs[-1].start()
    parts = []
    for b in range(blocks):
        span = slice(b * BLOCK_ROWS, (b + 1) * BLOCK_ROWS)
        low = low_v[b * RANK : (b + 1) * RANK, :].astype(BF16)
        parts.append(adapter_scale * dot(low, message_v[span, :]))
    part = jnp.concatenate(parts, axis=0)
    width = depth // groups
    lane = lax.broadcasted_iota(jnp.int32, (8, 128), 1) // width
    row = lax.broadcasted_iota(jnp.int32, (8, take), 0)
    turn = lax.broadcasted_iota(jnp.int32, (8, take), 1) // RANK % blocks
    slots = jnp.zeros((8, take), F32)
    for b in range(blocks):
        here = ((row == 0) & (turn == b)) | (row == 1 + b)
        slots = jnp.where(here, table_ref[ids_ref[0, b]].astype(F32), slots)
    fit = 128 // width
    for d in range(groups):
        column, mine = d // fit, d % fit
        halves = []
        for h in range(take // 128):
            total = jnp.zeros((8, 128), F32)
            for g in range(fit):
                k = h * fit + g
                tile = part[8 * k : 8 * k + 8, 128 * column : 128 * column + 128]
                tile = pltpu.roll(tile, ((g - mine) * width) % 128, 1)
                total = jnp.where(lane == g, tile, total)
            halves.append(total)
        packed = jnp.concatenate([jnp.concatenate(halves, axis=1), slots], axis=0)
        send_v[d, ranks:, :] = packed.astype(BF16)
    there = (pl.ds(0, groups), pl.ds(ranks, 16))
    outs.append(pltpu.make_async_copy(send_v.at[there], send_ref.at[there], out_sems.at[2 + chunks]))
    outs[-1].start()
    for out in outs:
        out.wait()


def front(count, ids, table, grad, up, acts, down, groups):
    blocks = count.shape[1]
    rows, width = acts.shape
    depth = grad.shape[1]
    wide = depth
    chunks = width // wide
    ranks = blocks * RANK
    shape = jax.ShapeDtypeStruct
    hbm = pl.BlockSpec(memory_space=HBM)
    send = shape((groups, ranks + 16, width // groups), BF16)
    return pl.pallas_call(
        front_kernel,
        out_shape=(
            HBM((EARLY, depth), BF16),
            HBM((rows + RANK - EARLY + chunks * ranks, depth), BF16),
            HBM(send.shape, BF16),
        ),
        in_specs=[hbm] * 7,
        out_specs=(hbm,) * 3,
        scratch_shapes=[
            pltpu.SMEM(count.shape, jnp.int32),
            pltpu.SMEM(ids.shape, jnp.int32),
            pltpu.SMEM(table.shape, jnp.int32),
            pltpu.VMEM((rows, depth), BF16),
            pltpu.VMEM((ranks, depth), BF16),
            pltpu.VMEM((chunks, rows, wide), BF16),
            pltpu.VMEM((chunks, ranks, wide), BF16),
            pltpu.VMEM((ranks, BLOCK_ROWS), F32),
            pltpu.VMEM((rows + RANK, depth), BF16),
            pltpu.VMEM(send.shape, BF16),
            pltpu.SemaphoreType.DMA((5,)),
            pltpu.SemaphoreType.DMA((chunks,)),
            pltpu.SemaphoreType.DMA((chunks,)),
            pltpu.SemaphoreType.DMA((chunks + 3,)),
            pltpu.SemaphoreType.DMA((chunks,)),
        ],
        compiler_params=vmem(18),
        cost_estimate=pl.CostEstimate(flops=10**10, transcendentals=0, bytes_accessed=3 * rows * width),
        name="front",
    )(*in_hbm(count, ids, table, grad, up, acts, down))


def join_kernel(counts, spots_ref, *refs):
    parts, outs, sems = refs[: sum(counts)], refs[sum(counts) : -1], refs[-1]
    copies = []
    for n, out in zip(counts, outs):
        for _ in range(n):
            i = len(copies)
            rows = parts[i].shape[0]
            at = pl.multiple_of(spots_ref[i] * rows, rows)
            copies.append(pltpu.make_async_copy(parts[i], out.at[pl.ds(at, rows)], sems.at[i]))
            copies[i].start()
    for copy in copies:
        copy.wait()


def join(spots, *groups, constrain):
    counts = tuple(len(g) for g in groups)
    in_vmem = pl.BlockSpec(memory_space=pltpu.VMEM)
    parts = [v for g in groups for v in g]
    if constrain:
        parts = in_hbm(*parts)
    return pl.pallas_call(
        functools.partial(join_kernel, counts),
        out_shape=[jax.ShapeDtypeStruct((sum(v.shape[0] for v in g), g[0].shape[1]), BF16) for g in groups],
        in_specs=[pl.BlockSpec(memory_space=pltpu.SMEM)] + [pl.BlockSpec(memory_space=HBM if constrain else pl.ANY)] * sum(counts),
        out_specs=[in_vmem] * len(groups),
        scratch_shapes=[pltpu.SemaphoreType.DMA((sum(counts),))],
        compiler_params=vmem(6),
        cost_estimate=pl.CostEstimate(flops=10**6, transcendentals=0, bytes_accessed=1 << 21),
        name="join",
    )(spots, *parts)


def collect_kernel(got_h, out_a, out_b, a_v, tail_v, pick_v, sems):
    sources, ranks, take = a_v.shape
    adapters = out_a.shape[0]
    blocks = ranks // RANK
    ins = [
        pltpu.make_async_copy(got_h.at[pl.ds(0, sources), pl.ds(ranks, 16)], tail_v, sems.at[0]),
        pltpu.make_async_copy(got_h.at[pl.ds(0, sources), pl.ds(0, ranks)], a_v, sems.at[1]),
    ]
    for copy in ins:
        copy.start()
    ins[0].wait()
    tail = tail_v[...].astype(F32)
    lane = lax.broadcasted_iota(jnp.int32, (RANK, 128), 1)
    same = lane % RANK == lax.broadcasted_iota(jnp.int32, (RANK, 128), 0)
    fit = 128 // ranks
    for v in range(sources // fit):
        slots = jnp.broadcast_to(tail[v * fit, 8:9, :128], (RANK, 128))
        for k in range(1, fit):
            row = jnp.broadcast_to(tail[v * fit + k, 8:9, :128], (RANK, 128))
            slots = jnp.where(lane // ranks == k, row, slots)
        slots = jnp.where(same, slots, -1.0)
        for j in range(adapters):
            pick = jnp.where(slots == float(j), 1.0, 0.0).astype(BF16)
            pick_v[j * RANK : (j + 1) * RANK, v * 128 : (v + 1) * 128] = pick
    ins[1].wait()
    total = dot(pick_v[...], a_v[...].reshape(sources * ranks, take))
    out_a[...] = total.reshape(adapters, RANK, take).astype(BF16)

    width = out_b.shape[1]
    terms = tail[:, :8, :].reshape(sources * 8, take).astype(BF16)
    lane = lax.broadcasted_iota(jnp.int32, (adapters, sources * 8), 1)
    slot = lax.broadcasted_iota(jnp.int32, (adapters, sources * 8), 0).astype(F32)
    sums = []
    for b in range(blocks):
        slots = jnp.zeros((1, sources * 8), F32)
        for source in range(sources):
            slots = jnp.where(lane[:1] // 8 == source, tail[source, 9 + b : 10 + b, : sources * 8], slots)
        hit = slots == slot
        pick = jnp.concatenate([jnp.where(hit & (lane % 8 == r), 1.0, 0.0) for r in range(8)], axis=0)
        at = b * 2 * width
        total = dot(pick.astype(BF16), terms[:, at // 128 * 128 : at // 128 * 128 + 128])
        sums.append(pltpu.roll(total, (128 - at % 128) % 128, 1))
    total = sums[0]
    for more in sums[1:]:
        total = total + more
    for r in range(8):
        turned = total[r * adapters : (r + 1) * adapters, :].T
        out_b[r] = turned[:width].astype(BF16)
        out_b[8 + r] = turned[width : 2 * width].astype(BF16)


def collect(got, adapters, blocks, depth):
    groups, _, take = got.shape
    ranks = blocks * RANK
    in_vmem = pl.BlockSpec(memory_space=pltpu.VMEM)
    return pl.pallas_call(
        collect_kernel,
        out_shape=(
            jax.ShapeDtypeStruct((adapters, RANK, take), BF16),
            jax.ShapeDtypeStruct((RANK, depth // groups, adapters), BF16),
        ),
        in_specs=[pl.BlockSpec(memory_space=HBM)],
        out_specs=(in_vmem, in_vmem),
        scratch_shapes=[
            pltpu.VMEM((groups, ranks, take), BF16),
            pltpu.VMEM((groups, 16, take), BF16),
            pltpu.VMEM((adapters * RANK, groups * ranks), BF16),
            pltpu.SemaphoreType.DMA((2,)),
        ],
        compiler_params=vmem(20),
        cost_estimate=pl.CostEstimate(flops=4 * 10**9, transcendentals=0, bytes_accessed=4 * got.size),
        name="collect",
    )(*in_hbm(got))


def unpack_kernel(early_ref, late_ref, message_ref, low_ref, down_ref):
    rows = message_ref.shape[0]
    ranks = low_ref.shape[1]
    rest = rows - EARLY
    message_ref[:EARLY, :] = early_ref[...]
    message_ref[EARLY:, :] = late_ref[:rest, :]
    down_ref[...] = late_ref[rest + RANK :, :]
    low = jnp.concatenate([late_ref[rest : rest + RANK, :rows].astype(F32)] * (ranks // RANK), axis=0)
    own = lax.broadcasted_iota(jnp.int32, low.shape, 0) // RANK
    of = lax.broadcasted_iota(jnp.int32, low.shape, 1) // BLOCK_ROWS
    low_ref[...] = jnp.where(own == of, low, 0.0).T.astype(BF16)


def unpack(early, late, rows, ranks):
    depth = early.shape[1]
    shape = jax.ShapeDtypeStruct
    in_vmem = pl.BlockSpec(memory_space=pltpu.VMEM)
    return pl.pallas_call(
        unpack_kernel,
        out_shape=(
            shape((rows, depth), BF16),
            shape((rows, ranks), BF16),
            shape((late.shape[0] + EARLY - rows - RANK, depth), BF16),
        ),
        in_specs=[in_vmem] * 2,
        out_specs=(in_vmem,) * 3,
        compiler_params=vmem(4),
        name="unpack",
    )(early, late)


def product_kernel(which, alias, starts_ref, message_ref, low_ref, down_ref, *refs):
    n = len(which)
    blocks = refs[:n]
    out_ref, out_v, out_sems = refs[n + alias :]
    ranks, wide = low_ref.shape[1], down_ref.shape[1]
    outs = []
    for i in range(n):
        start = pl.multiple_of(starts_ref[which[i]], BLOCK)
        chunk = pl.ds(pl.multiple_of(start // wide * ranks, ranks), ranks)
        down = down_ref[chunk, pl.ds(pl.multiple_of(start % wide, BLOCK), BLOCK)]
        total = dot(message_ref[...], blocks[i][...], LAST) + dot(low_ref[...], down)
        out_v[i] = total.astype(BF16)
        out = pltpu.make_async_copy(out_v.at[i], out_ref.at[:, pl.ds(start, BLOCK)], out_sems.at[i])
        out.start()
        outs.append(out)
    for out in outs:
        out.wait()


def product(blocks, starts, message, low, down, before, name):
    n = len(blocks)
    rows, depth = message.shape
    width = down.size // low.shape[1]
    operands = [starts, message, low, down, *[b[0] for b in blocks]]
    in_vmem = pl.BlockSpec(memory_space=pltpu.VMEM)
    in_specs = [pl.BlockSpec(memory_space=pltpu.SMEM)] + [in_vmem] * (len(operands) - 1)
    hbm = pl.BlockSpec(memory_space=HBM)
    if before is not None:
        operands += in_hbm(before)
        in_specs.append(hbm)
    columns = n * BLOCK
    return pl.pallas_call(
        functools.partial(product_kernel, tuple(b[1] for b in blocks), before is not None),
        out_shape=jax.ShapeDtypeStruct((rows, width), BF16),
        in_specs=in_specs,
        out_specs=hbm,
        scratch_shapes=[pltpu.VMEM((n, rows, BLOCK), BF16), pltpu.SemaphoreType.DMA((n,))],
        input_output_aliases={} if before is None else {len(operands) - 1: 0},
        compiler_params=vmem(12),
        cost_estimate=pl.CostEstimate(
            flops=10**6, transcendentals=0, bytes_accessed=10**6
        ),
        name=name,
    )(*operands)


def spot(at, core):
    return (at + core) % SIDE


def near(at, core):
    return ((spot(at, core) ^ 1) - core) % SIDE


def far(at, core):
    return (SIDE - 1 - spot(at, core) - core) % SIDE


def moved(array, to):
    route = []
    for d in range(SIDE * SIDE * CORES):
        x, z, core = to(d // (SIDE * CORES), d // CORES % SIDE, d % CORES)
        route.append((d, (x * SIDE + z) * CORES + core))
    return lax.ppermute(array, "dp", route)


def x_near(x, z, core):
    return near(x, core), z, core


def x_far(x, z, core):
    return far(x, core), z, core


def z_near(x, z, core):
    return x, near(z, core), core


def z_far(x, z, core):
    return x, far(z, core), core


def other_core(x, z, core):
    return x, z, 1 - core


def places(line, core):
    steps = (line, near(line, core), far(line, core), near(far(line, core), core))
    return [(s * CORES + core) * BLOCK for s in steps]


def hop(x, route):
    return lax.ppermute(x, "pipe", route)


def tie(*arrays):
    return lax.optimization_barrier(arrays)


def body(
    acts,
    output_gradient,
    frozen_value_weight,
    adapter_down_weight,
    adapter_up_weight,
    block_adapter_index,
    token_row_count,
    adapter_slot_table,
):
    blocks = token_row_count.shape[1]
    rows, width = acts.shape[1:]
    depth = output_gradient.shape[2]
    adapters = adapter_slot_table.shape[0]
    groups = lax.axis_size("dp")
    down = adapter_down_weight.reshape(blocks * RANK, width)
    up = adapter_up_weight.reshape(blocks * RANK, depth)
    half = width // 2
    me = lax.axis_index("dp")
    x, z, core = me // (SIDE * CORES), me // CORES % SIDE, me % CORES
    back = [(1, 0), (2, 1), (3, 2)]

    piece_a = lax.dynamic_slice_in_dim(
        frozen_value_weight[0], ((z * CORES + core) * SIDE + spot(x, core)) * PIECE, PIECE, 0
    )
    piece_b = lax.dynamic_slice_in_dim(
        frozen_value_weight[0], half + ((x * CORES + core) * SIDE + spot(z, core)) * PIECE, PIECE, 0
    )
    a0, b0 = hop(piece_a, back), hop(piece_b, back)
    early, late, send = front(
        token_row_count, block_adapter_index, adapter_slot_table,
        output_gradient[0], up, acts[0], down, groups,
    )
    spot_a, spot_b = spot(x, core), spot(z, core)
    halves_a = jnp.stack([spot_a % 2, 1 - spot_a % 2]).astype(jnp.int32)
    halves_b = jnp.stack([spot_b % 2, 1 - spot_b % 2]).astype(jnp.int32)
    wholes = jnp.stack([spot_a // 2, 1 - spot_a // 2, spot_b // 2, 1 - spot_b // 2]).astype(jnp.int32)
    starts = []
    for c in (core, 1 - core):
        starts += places(z, c) + [half + s for s in places(x, c)]
    starts = jnp.stack(starts).astype(jnp.int32)
    a0, b0, send, early, late, halves_a, halves_b, wholes, starts = tie(
        a0, b0, send, early, late, halves_a, halves_b, wholes, starts
    )

    a1, b1 = moved(a0, x_near), moved(b0, z_near)
    early = hop(early, back)
    b0, b1, send, late = tie(b0, b1, send, late)

    got = lax.all_to_all(send, "dp", split_axis=0, concat_axis=0, tiled=True)
    ap, = join(halves_a, (a0, a1), constrain=False)
    bp, = join(halves_b, (b0, b1), constrain=False)
    aq, bq = moved(ap, x_far), moved(bp, z_far)
    aq, bq, early, late = tie(aq, bq, early, late)

    late = hop(late, back)
    a, b = join(wholes, (ap, aq), (bp, bq), constrain=True)
    a_near, b_near = moved(a, z_near), moved(b, x_near)
    a_far, b_far = moved(a, z_far), moved(b, x_far)
    total_a, total_b = collect(got, adapters, blocks, depth)
    a, b, a_near, b_near, total_a, total_b = tie(a, b, a_near, b_near, total_a, total_b)

    def pair(a, b, step, mine=True):
        at = step if mine else step + 2 * SIDE
        return [(a, at), (b, at + SIDE)]

    def others(a, b, step):
        return pair(moved(a, other_core), moved(b, other_core), step, False)

    a_last, b_last = moved(a_near, z_far), moved(b_near, x_far)
    late, a_far, b_far = tie(late, a_far, b_far)
    message, low, down = unpack(early, late, rows, blocks * RANK)
    message, a, b, a_near = tie(message, a, b, a_near)
    shared = (starts, message, low, down)
    mine = pair(a, b, 0) + pair(a_near, b_near, 1) + pair(a_far, b_far, 2)
    received = product(mine, *shared, None, "product_mine")
    a_other, b_other, a_near_other = [moved(v, other_core) for v in (a, b, a_near)]
    received, a_other, b_other, a_near_other, b_near, a_far, b_far = tie(
        received, a_other, b_other, a_near_other, b_near, a_far, b_far
    )
    first = pair(a_other, b_other, 0, False) + [(a_near_other, 1 + 2 * SIDE)]
    second = [(moved(b_near, other_core), 1 + 3 * SIDE)] + others(a_far, b_far, 2)
    received = product(first, *shared, received, "product_first")
    received, a_last, b_last = tie(received, a_last, b_last)
    theirs = others(a_last, b_last, 3)
    received = product(second + pair(a_last, b_last, 3), *shared, received, "product_second")
    received = product(theirs, *shared, received, "product_end")
    return received[None], total_a[None], jnp.transpose(total_b, (2, 0, 1))[None]


def solution(mesh):
    in_specs = (
        P("pipe", "dp", None),
        P("pipe", "dp", None),
        P("pipe", None, None),
        P("pipe", "dp", None, None),
        P("pipe", "dp", None, None),
        P("pipe", "dp"),
        P("pipe", "dp"),
        P(),
    )
    out_specs = (P("pipe", "dp", None), P("pipe", None, None, "dp"), P("pipe", None, None, "dp"))
    return jax.shard_map(body, mesh=mesh, in_specs=in_specs, out_specs=out_specs, check_vma=False)
```
